512 devices in a mesh: slab: 128 (over z_lo, x, y), cross: 4 (over z_hi, core).
Axes of the slice: x: 4, y: 8, z: 8 (z_hi: 2, z_lo: 4; z = z_hi * 4 + z_lo), core: 2. Of those that a mesh axis runs over, the one named last changes fastest.
Arguments:
- populations: float32 [19, 512, 32, 128], P(None, 'slab', 'cross'), may hold values from 0 to 1, as said below
- fluid_mask: int32 [512, 32, 128], P('slab', 'cross'), may hold values 0 or 1
- relaxation: float32 [512, 32, 128], P('slab', 'cross'), may hold values from 0.8 to 1.7
- positions: int32 [3, 2048, 642], P(None, 'slab'), may hold values from -1 to 512, as said below
- triangles: int32 [3, 1280], replicated, may hold values from 0 to 641, as said below
- tension: float32 [2048, 1280], P('slab'), may hold values from 0.0003 to 0.003
- coarse_moments: float32 [4, 65536], P(None, 'slab'), may hold values from -0.2 to 1.2, as said below
- interface: int32 [3, 65536], P(None, ('slab', 'cross')), may hold values from -1 to 65535, as said below
Outputs:
- populations_next: float32 [19, 512, 32, 128], P(None, 'slab', 'cross')
- flow: float32 [3, 512, 32, 128], P(None, 'slab', 'cross')
The draws below stay inside these ranges and needn't reach their ends.
Inputs may be any that keep to these rules, and one draw needn't show every extreme that they name: `positions`: nodes of membrane m lie in planes 4 * (m // 16) - 1 to 4 * (m // 16) + 4, columns 0 to 31 and rows 0 to 127. `triangles`: each triangle names three different nodes of a membrane. `interface`: in each block of 128 columns (one device's, slab major), row 0 names different cells of that device's block, numbered (plane * 8 + column) * 128 + row, or -1 for an unused slot; rows 1 and 2 name coarse cells. `populations`: populations are positive. `coarse_moments`: row 0 is a positive density, rows 1 to 3 a velocity.
All inputs are finite; a program needn't handle non-finite values. No bound on the sum of `fluid_mask` on one device may be relied on, other than what follows from the above.
Results may differ from the reference program's by a relative error of at most 0.0001.
Values sent between devices are 32-bit elements; how exact they have to be, the bound alone decides.
No kernel may reach another device: no remote copies, remote signals or barrier semaphores. Data moves between devices by JAX's collectives and lax.ppermute only.
A program may use at most 128 MiB of HBM per device.

```python
import math
import jax
import jax.numpy as jnp
import numpy as np
from jax import lax

PL = 4
SX = 8
NY = 128
MEMB_DEV = 16
MNODES = 642
MTRI = 1280
IF_DEV = 128
STEPS = 4
NZ = 512
NX = 32
MEMBS = 2048
NCOARSE = 65536
IFACES = 65536


LATTICE_VECTORS = [(0, 0, 0), (1, 0, 0), (-1, 0, 0), (0, 1, 0), (0, -1, 0), (0, 0, 1), (0, 0, -1), (1, 1, 0), (-1, -1, 0), (1, -1, 0), (-1, 1, 0), (1, 0, 1), (-1, 0, -1), (1, 0, -1), (-1, 0, 1), (0, 1, 1), (0, -1, -1), (0, 1, -1), (0, -1, 1)]


LATTICE_WEIGHTS = [1.0 / 3.0] + [1.0 / 18.0] * 6 + [1.0 / 36.0] * 12


def equilibrium_draw(density, velocity):
    squared = velocity[0] * velocity[0] + velocity[1] * velocity[1] + velocity[2] * velocity[2]
    planes = []
    for member, vector in enumerate(LATTICE_VECTORS):
        projected = vector[0] * velocity[0] + vector[1] * velocity[1] + vector[2] * velocity[2]
        planes.append(LATTICE_WEIGHTS[member] * density * (1.0 + 3.0 * projected + 4.5 * projected * projected - 1.5 * squared))
    return jnp.stack(planes)


def draw_populations(key, part):
    subkeys = jax.random.split(jax.random.fold_in(key, 3), 3)
    grid = (NZ, NX, NY)
    density = jax.random.uniform(subkeys[0], grid, jnp.float32, 0.9, 1.1)
    velocity = jnp.clip(0.05 * jax.random.normal(subkeys[1], (3,) + grid, jnp.float32), -0.15, 0.15)
    spread = 0.1
    noise = jax.random.uniform(subkeys[2], (19,) + grid, jnp.float32, -1.0, 1.0)
    return equilibrium_draw(density, velocity) * (1.0 + spread * noise)


def draw_coarse_moments(key, part):
    subkeys = jax.random.split(jax.random.fold_in(key, 4), 2)
    density = jax.random.uniform(subkeys[0], (1, NCOARSE), jnp.float32, 0.9, 1.1)
    velocity = jnp.clip(0.05 * jax.random.normal(subkeys[1], (3, NCOARSE), jnp.float32), -0.15, 0.15)
    return jnp.concatenate([density, velocity], axis=0)


def draw_positions(key, part):
    subkeys = jax.random.split(jax.random.fold_in(key, 5), 5)
    membrane = jnp.arange(MEMBS, dtype=jnp.int32)[:, None]
    slab_owner = membrane // MEMB_DEV
    plane_ids = slab_owner * PL - 1 + jax.random.randint(subkeys[0], (MEMBS, MNODES), 0, PL + 2)
    centre_column = jax.random.randint(subkeys[1], (MEMBS, 1), 3, NX - 3)
    column_ids = jnp.clip(centre_column + jax.random.randint(subkeys[2], (MEMBS, MNODES), -3, 4), 0, NX - 1)
    centre_row = jax.random.randint(subkeys[3], (MEMBS, 1), 3, NY - 3)
    row_ids = centre_row + jax.random.randint(subkeys[4], (MEMBS, MNODES), -3, 4)
    return jnp.stack([plane_ids, column_ids, row_ids]).astype(jnp.int32)


def draw_triangles(key, part):
    subkeys = jax.random.split(jax.random.fold_in(key, 7), 3)
    vertex_one = jax.random.randint(subkeys[0], (MTRI,), 0, MNODES)
    step_one = jax.random.randint(subkeys[1], (MTRI,), 1, MNODES)
    step_two = jax.random.randint(subkeys[2], (MTRI,), 1, MNODES - 1)
    step_two = step_two + (step_two >= step_one).astype(jnp.int32)
    return jnp.stack([vertex_one, (vertex_one + step_one) % MNODES, (vertex_one + step_two) % MNODES]).astype(jnp.int32)


def draw_interface(key, part):
    subkeys = jax.random.split(jax.random.fold_in(key, 9), 5)
    devices = IFACES // IF_DEV
    cell_total = PL * SX * NY

    def choose_cells(device_key):
        return jax.random.permutation(device_key, cell_total)[:IF_DEV]
    chosen = jax.vmap(choose_cells)(jax.random.split(subkeys[0], devices))
    counts = jax.random.randint(subkeys[1], (devices,), max(IF_DEV // 4, 1), IF_DEV + 1)
    fullest = jax.random.randint(subkeys[2], (), 0, devices)
    counts = jnp.where(jnp.arange(devices, dtype=jnp.int32) == fullest, IF_DEV, counts)
    slots = jnp.arange(IF_DEV, dtype=jnp.int32)
    cell_ids = jnp.where(slots[None, :] < counts[:, None], chosen, -1).reshape(-1)
    coarse_one = jax.random.randint(subkeys[3], (IFACES,), 0, NCOARSE)
    coarse_two = jax.random.randint(subkeys[4], (IFACES,), 0, NCOARSE)
    return jnp.stack([cell_ids, coarse_one, coarse_two]).astype(jnp.int32)


def touch_ends(entries, stream_key, least, high):
    longest = entries.shape.index(max(entries.shape))
    spots = []
    for shift in (0, 1):
        where = [jax.random.randint(jax.random.fold_in(stream_key, axis), (), 0, length) for axis, length in enumerate(entries.shape)]
        where[longest] = (where[longest] + shift) % entries.shape[longest]
        spots.append(tuple(where))
    return entries.at[spots[0]].set(least).at[spots[1]].set(high)


def steps_of(rng, extent, shards, smallest, top_value):
    def one(axis_at, blocks):
        heights = jax.random.uniform(jax.random.fold_in(jax.random.fold_in(rng, 6), axis_at), (blocks,), jnp.float32, smallest / len(shards), top_value / len(shards))
        return jnp.repeat(jnp.exp(heights), extent[axis_at] // blocks).reshape((-1,) + (1,) * (len(extent) - axis_at - 1))

    gain = one(*shards[0])
    for cut in shards[1:]:
        gain = gain * one(*cut)
    return gain


def setup_inputs(seed: int = 0) -> dict:
    streams_of = jax.random.split(jax.random.key(seed), 9)
    populations = draw_populations(jax.random.fold_in(streams_of[8], 71), 0)
    fluid_mask = touch_ends((jax.random.randint(streams_of[1], (NZ, NX, NY), 0, 8) < 7).astype(jnp.int32), jax.random.fold_in(streams_of[1], 1), 0, 1)
    relaxation = jnp.clip(jnp.exp(math.log(1.7) - 0.75377182 * jax.random.uniform(streams_of[2], (NZ, NX, NY), jnp.float32) ** steps_of(streams_of[2], (NZ, NX, NY), ((0, 128), (1, 4)), -0.2, 0.2)), 0.8, 1.7)
    positions = draw_positions(jax.random.fold_in(streams_of[8], 71), 0)
    triangles = draw_triangles(jax.random.fold_in(streams_of[8], 71), 0)
    tension = jnp.clip(jnp.exp(math.log(0.003) - 2.3025851 * jax.random.uniform(streams_of[5], (MEMBS, MTRI), jnp.float32) ** steps_of(streams_of[5], (MEMBS, MTRI), ((0, 128),), -0.2, 0.2)), 0.0003, 0.003)
    coarse_moments = draw_coarse_moments(jax.random.fold_in(streams_of[8], 71), 0)
    interface = draw_interface(jax.random.fold_in(streams_of[8], 71), 0)
    return {"populations": populations, "fluid_mask": fluid_mask, "relaxation": relaxation, "positions": positions, "triangles": triangles, "tension": tension, "coarse_moments": coarse_moments, "interface": interface}


LATTICE_VECTORS = [(0, 0, 0), (1, 0, 0), (-1, 0, 0), (0, 1, 0), (0, -1, 0), (0, 0, 1), (0, 0, -1), (1, 1, 0), (-1, -1, 0), (1, -1, 0), (-1, 1, 0), (1, 0, 1), (-1, 0, -1), (1, 0, -1), (-1, 0, 1), (0, 1, 1), (0, -1, -1), (0, 1, -1), (0, -1, 1)]
LATTICE_WEIGHTS = [1.0 / 3.0] + [1.0 / 18.0] * 6 + [1.0 / 36.0] * 12
OPPOSITE = [0] + [member + 1 if member % 2 == 1 else member - 1 for member in range(1, 19)]
ROOT_THREE = math.sqrt(3.0)

def equilibrium(density, velocity):
    lattice = jnp.asarray(LATTICE_VECTORS, jnp.float32)
    weights = jnp.asarray(LATTICE_WEIGHTS, jnp.float32).reshape((19,) + (1,) * density.ndim)
    projected = jnp.einsum('qk,k...->q...', lattice, velocity, precision=lax.Precision.HIGHEST)
    squared = lax.optimization_barrier(jnp.sum(velocity * velocity, axis=0))
    return weights * density * (1.0 + 3.0 * projected + 4.5 * projected * projected - 1.5 * squared)

def moments(fields):
    lattice = jnp.asarray(LATTICE_VECTORS, jnp.float32)
    density = lax.optimization_barrier(jnp.sum(fields, axis=0))
    momentum = jnp.einsum('qk,q...->k...', lattice, fields, precision=lax.Precision.HIGHEST)
    return (density, momentum)

def collide(fields, body_force, relaxation, fluid_mask):
    density, momentum = moments(fields)
    shifted = momentum / density + body_force / (relaxation * density)
    relaxed = fields + relaxation * (equilibrium(density, shifted) - fields)
    reversed_fields = fields[np.array(OPPOSITE)]
    return jnp.where(fluid_mask[None] == 1, relaxed, reversed_fields)

def stream(padded, plane_count, column_count):
    wrapped = jnp.concatenate([padded[..., -1:], padded, padded[..., :1]], axis=-1)
    across = padded.shape[-1]
    planes = []
    for member, vector in enumerate(LATTICE_VECTORS):
        step_plane, step_column, step_row = vector
        planes.append(wrapped[member, 1 - step_plane:1 - step_plane + plane_count, 1 - step_column:1 - step_column + column_count, 1 - step_row:1 - step_row + across])
    return jnp.stack(planes)

def node_force(positions, triangles, tension):
    coords = positions.astype(jnp.float32)
    vertex_one = coords[:, :, triangles[0]]
    vertex_two = coords[:, :, triangles[1]]
    vertex_three = coords[:, :, triangles[2]]
    scaled = tension[None]
    running = jnp.zeros(coords.shape, jnp.float32)
    running = running.at[:, :, triangles[0]].add(scaled * (vertex_two + vertex_three - 2.0 * vertex_one))
    running = running.at[:, :, triangles[1]].add(scaled * (vertex_one + vertex_three - 2.0 * vertex_two))
    running = running.at[:, :, triangles[2]].add(scaled * (vertex_one + vertex_two - 2.0 * vertex_three))
    return running

def spread_global(positions, nodal_force):
    force_field = jnp.zeros((3, NZ + 4, NX + 2, NY), jnp.float32)
    kernel = (0.25, 0.5, 0.25)
    for offset_plane in (-1, 0, 1):
        for offset_column in (-1, 0, 1):
            for offset_row in (-1, 0, 1):
                weight = kernel[offset_plane + 1] * kernel[offset_column + 1] * kernel[offset_row + 1]
                plane_ids = positions[0] + 2 + offset_plane
                column_ids = positions[1] + 1 + offset_column
                row_ids = (positions[2] + offset_row) % NY
                force_field = force_field.at[:, plane_ids, column_ids, row_ids].add(weight * nodal_force)
    return force_field[:, 2:NZ + 2, 1:NX + 1]

def reference(populations, fluid_mask, relaxation, positions, triangles, tension, coarse_moments, interface):
    body_force = spread_global(positions, node_force(positions, triangles, tension))
    blended = 0.75 * coarse_moments[:, interface[1]] + 0.25 * coarse_moments[:, interface[2]]
    boundary = equilibrium(blended[0], blended[1:4])
    local_cell = interface[0]
    device = jnp.arange(IFACES, dtype=jnp.int32) // IF_DEV
    crosses = NX // SX
    slab_owner = device // crosses
    cross_owner = device % crosses
    plane_ids = slab_owner * PL + local_cell // (SX * NY)
    column_ids = cross_owner * SX + local_cell // NY % SX
    row_ids = local_cell % NY
    target = jnp.where(local_cell >= 0, (plane_ids * NX + column_ids) * NY + row_ids, NZ * NX * NY).astype(jnp.int32)
    fields = populations
    for iteration in range(STEPS):
        relaxed = collide(fields, body_force, relaxation, fluid_mask)
        padded = jnp.pad(relaxed, ((0, 0), (1, 1), (1, 1), (0, 0)))
        passed = stream(padded, NZ, NX)
        fields = passed.reshape(19, -1).at[:, target].set(boundary, mode='drop').reshape(passed.shape)
    density, momentum = moments(fields)
    return (fields, ROOT_THREE * momentum / density)
```

```python
import math

import jax
import jax.numpy as jnp
from jax import lax
from jax.experimental import pallas as pl
from jax.experimental.pallas import tpu as pltpu
from jax.sharding import PartitionSpec as P

F32 = jnp.float32
BF16 = jnp.bfloat16
I32 = jnp.int32
ROOT_THREE = math.sqrt(3.0)
VELOCITIES = [
    (0, 0, 0),
    (1, 0, 0),
    (-1, 0, 0),
    (0, 1, 0),
    (0, -1, 0),
    (0, 0, 1),
    (0, 0, -1),
    (1, 1, 0),
    (-1, -1, 0),
    (1, -1, 0),
    (-1, 1, 0),
    (1, 0, 1),
    (-1, 0, -1),
    (1, 0, -1),
    (-1, 0, 1),
    (0, 1, 1),
    (0, -1, -1),
    (0, 1, -1),
    (0, -1, 1),
]
STEPS = 4
PLANES = 4
COLUMNS = 8
ROWS = 128
DEEP = PLANES + 2 * STEPS
WIDE = COLUMNS + 2 * STEPS
CROSS = 4
GROUP = 32
MASKS = (4, 16, 2, 1, 8)
NODES = 768
MEMBRANES = 16
VMEM_LIMIT = 56 * 1024 * 1024


def call(body, outs, scratch=(), flops=0, **more):
    return pl.pallas_call(
        body,
        out_shape=outs,
        scratch_shapes=list(scratch),
        compiler_params=pltpu.CompilerParams(vmem_limit_bytes=VMEM_LIMIT),
        cost_estimate=pl.CostEstimate(flops=flops, bytes_accessed=1 << 20, transcendentals=0),
        **more,
    )


def struct(*shape, dtype=F32):
    return jax.ShapeDtypeStruct(shape, dtype)


def pack_kernel(pops, relax, mask, iface, coarse, own_o, right_o, left_o, iface_o, coarse_o):
    def put(field, z, value):
        own_o[field * 4 + z] = value
        low = (z % 2) * 4
        right_o[field * 2 + z // 2, low : low + 4] = value[4:8]
        left_o[field * 2 + z // 2, low : low + 4] = value[0:4]

    for z in range(PLANES):
        for q in range(19):
            put(q, z, pops[q, z])
        put(19, z, relax[z])
        put(20, z, mask[z].astype(F32))
    tile = jnp.zeros((8, ROWS), F32)
    iface_o[...] = tile
    iface_o[0:3] = iface[...].astype(F32)
    right_o[42] = iface_o[...]
    left_o[42] = iface_o[...]
    for sub in range(4):
        for mom in range(4):
            coarse_o[sub : sub + 1, mom * 128 : (mom + 1) * 128] = coarse[
                mom : mom + 1, sub * 128 : (sub + 1) * 128
            ]


def halo_kernel(from_left, from_right, iface_far, iface_own, halo_o):
    k = lax.axis_index("cross")
    has_right = jnp.where(k < CROSS - 1, 1.0, 0.0).astype(F32)
    has_left = jnp.where(k > 0, 1.0, 0.0).astype(F32)
    for tile in range(42):
        right = from_right[tile] * has_right
        left = from_left[tile] * has_left
        halo_o[2 * tile, 0:4] = right[0:4]
        halo_o[2 * tile + 1, 0:4] = right[4:8]
        halo_o[2 * tile, 4:8] = left[0:4]
        halo_o[2 * tile + 1, 4:8] = left[4:8]
    halo_o[84 + k] = iface_own[...]
    halo_o[84 + (k + 1) % 4] = from_right[42]
    halo_o[84 + (k + 3) % 4] = from_left[42]
    halo_o[84 + (k + 2) % 4] = iface_far[...]


def nodal_kernel(positions, triangles, tension, out, x_s, table_s):
    j = lax.axis_index("slab")
    k = lax.axis_index("cross")
    x_s[...] = jnp.zeros_like(x_s)
    for d in range(3):
        coords = positions[d].astype(F32)
        x_s[d * 16 : d * 16 + 16, 0:642] = coords - coords[:, 0:1]
    tri = triangles[...]
    for low in range(0, NODES, 128):
        ids = lax.broadcasted_iota(I32, (128, 1280), 0) + low
        hit = (ids == tri[0:1]) | (ids == tri[1:2]) | (ids == tri[2:3])
        table_s[low : low + 128] = jnp.where(hit, 1.0, 0.0).astype(BF16)
    x = x_s[...]
    table = table_s[...]
    corners = jnp.dot(x.astype(BF16), table, preferred_element_type=F32)
    s = tension[...]
    weighted = jnp.concatenate([corners[d * 16 : d * 16 + 16] * s for d in range(3)] + [s], axis=0)
    high = weighted.astype(BF16)
    rest = weighted - high.astype(F32)
    middle = rest.astype(BF16)
    low_part = (rest - middle.astype(F32)).astype(BF16)
    stacked = jnp.concatenate([high, middle, low_part], axis=0)
    sums = lax.dot_general(stacked, table, (((1,), (1,)), ((), ())), preferred_element_type=F32)
    total = sums[0:64] + sums[64:128] + sums[128:192]
    out[...] = jnp.zeros_like(out)
    base = (j * PLANES, k * COLUMNS, 0)
    for d in range(3):
        force = total[d * 16 : d * 16 + 16] - 3.0 * x[d * 16 : d * 16 + 16] * total[48:64]
        place = (positions[d] - base[d]).astype(F32)
        for m in range(MEMBRANES):
            out[m, d : d + 1] = force[m : m + 1]
            out[m, 3 + d : 4 + d, 0:642] = place[m : m + 1]


def spread_body(nodes, initial, finished):
    plane_ids = lax.broadcasted_iota(I32, (8, NODES), 0).astype(F32) - 2.0
    column_ids = lax.broadcasted_iota(I32, (WIDE, NODES), 0)
    column_ids = jnp.where(column_ids < 12, column_ids, column_ids - 16).astype(F32)
    row_ids = (lax.broadcasted_iota(I32, (ROWS, NODES), 0).astype(F32) * 0.25).astype(BF16)

    def add(m, running):
        node = nodes[m]
        along_plane = jnp.maximum(0.5 - 0.25 * jnp.abs(plane_ids - node[3:4]), 0.0)
        along_column = jnp.maximum(0.5 - 0.25 * jnp.abs(column_ids - node[4:5]), 0.0)
        row = jnp.broadcast_to(node[5:6] * 0.25, (16, NODES)).astype(BF16)
        row = jnp.concatenate([row] * 8, axis=0)
        along_row = jnp.abs(jnp.abs(row_ids - row) - BF16(16.0))
        along_row = jnp.maximum(along_row - BF16(15.5), BF16(0.0))
        parts = []
        rest = []
        for d in range(3):
            high = node[d : d + 1].astype(BF16).astype(F32)
            parts.append((high * along_column).astype(BF16))
            rest.append(((node[d : d + 1] - high).astype(BF16).astype(F32) * along_column).astype(BF16))
        block = jnp.concatenate(parts + rest, axis=0)
        stacked = []
        for p in range(8):
            weight = jnp.broadcast_to(along_plane[p : p + 1], (16, NODES)).astype(BF16)
            stacked.append(block * jnp.concatenate([weight] * 6, axis=0))
        lhs = jnp.concatenate(stacked, axis=0)
        return running + lax.dot_general(
            lhs, along_row, (((1,), (1,)), ((), ())), preferred_element_type=F32
        )

    return lax.fori_loop(0, nodes.shape[0], add, initial)


def spread_first_kernel(nodes, out):
    out[...] = spread_body(nodes, jnp.zeros((768, ROWS), F32), None)


def spread_last_kernel(nodes, partial, own_o, up_o, down_o, up2_o, down2_o):
    total = spread_body(nodes, partial[...], None)
    for p in range(8):
        for d in range(3):
            low = p * 96 + d * 16
            value = total[low : low + 16] + total[low + 48 : low + 64]
            own_o[p, d] = value
            if p >= 2:
                up_o[p - 2, d] = value
            if p < 6:
                down_o[p, d] = value
            if p >= 6:
                up2_o[p - 6, d] = value
            if p < 2:
                down2_o[p, d] = value


def lookup_kernel(first, second, up, own, down, out):
    k = lax.axis_index("cross")
    place = lax.rem(lax.axis_index("slab"), GROUP)
    table = jnp.concatenate([first[...], second[...]], axis=0).T
    high = table.astype(BF16)
    low = (table - high.astype(F32)).astype(BF16)
    lhs = jnp.concatenate([high, low], axis=1)
    ids = lax.broadcasted_iota(I32, (128, 256), 0)
    for d, source in enumerate((up, own, down)):
        for a in range(CROSS):
            tile = source[a].astype(I32)
            cell = jnp.concatenate([tile[1:2], tile[2:3]], axis=1)
            shard = cell >> 9
            apart = (shard & (GROUP - 1)) ^ place
            block = jnp.zeros_like(cell)
            for bit, mask in enumerate(MASKS):
                block = block + jnp.where((apart & mask) != 0, 1 << bit, 0)
            row = block * 4 + ((cell >> 7) & 3)
            row = jnp.where((shard >> 5) == k, row, -1)
            lane = cell & 127
            hot = jnp.where(ids == row, 1.0, 0.0).astype(BF16)
            found = jnp.dot(
                lhs, jnp.concatenate([hot, hot], axis=0), preferred_element_type=F32
            )
            chosen = ids == lane
            for mom in range(4):
                value = jnp.sum(
                    jnp.where(chosen, found[mom * 128 : mom * 128 + 128], 0.0), axis=0, keepdims=True
                )
                at = (d * CROSS + a) * 4 + mom
                out[at : at + 1] = 0.75 * value[:, 0:128] + 0.25 * value[:, 128:256]


def rolled(value, velocity):
    if velocity[1]:
        value = pltpu.roll(value, velocity[1] % WIDE, 0)
    if velocity[2]:
        value = pltpu.roll(value, velocity[2] % ROWS, 1)
    return value


def moments(fields):
    def pick(d, sign):
        return [f for f, c in zip(fields, VELOCITIES) if c[d] == sign]

    def add(values):
        while len(values) > 1:
            values = [a + b for a, b in zip(values[::2], values[1::2])] + (
                [values[-1]] if len(values) % 2 else []
            )
        return values[0]

    return add(list(fields)), [add(pick(d, 1)) - add(pick(d, -1)) for d in range(3)]


def equilibrium_terms(v):
    base = 1.0 - 1.5 * (v[0] * v[0] + v[1] * v[1] + v[2] * v[2])
    t = [3.0 * x for x in v]
    pairs = []
    for q in range(1, 19, 2):
        c = VELOCITIES[q]
        along = None
        for d in range(3):
            if c[d]:
                term = t[d]
                if along is None:
                    along = term
                else:
                    along = along + term if c[d] == 1 else along - term
        pairs.append((along, base + 0.5 * along * along))
    return base, pairs


def steps_kernel(
    pops, relax, mask, up, down, halo, halo_up, halo_down,
    force, force_m1, force_p1, force_m2, force_p2, v0, v1, v2, v3,
    pops_o, flow_o,
    f_s, g_s, edge_s, hit_s, relax_s, mask_s, force_s, dense_s,
):
    j = lax.axis_index("slab")
    k = lax.axis_index("cross")
    slabs = lax.axis_size("slab")
    for q in range(19):
        span = slice(q * 4, q * 4 + 4)
        f_s[q, 5:9, 0:8] = pops[q]
        f_s[q, 5:9, 8:16] = halo[span]
        f_s[q, 1:5, 0:8] = up[span]
        f_s[q, 1:5, 8:16] = halo_up[span]
        f_s[q, 9:13, 0:8] = down[span]
        f_s[q, 9:13, 8:16] = halo_down[span]
    for field, dest in ((19, relax_s), (20, mask_s)):
        span = slice(field * 4, field * 4 + 4)
        dest[4:8, 0:8] = relax[...] if field == 19 else mask[...].astype(F32)
        dest[4:8, 8:16] = halo[span]
        dest[0:4, 0:8] = up[span]
        dest[0:4, 8:16] = halo_up[span]
        dest[8:12, 0:8] = down[span]
        dest[8:12, 8:16] = halo_down[span]
    for p in range(DEEP):
        inverse = 1.0 / relax_s[p]
        for d in range(3):
            value = None
            for part, low in ((force, 2), (force_m1, 0), (force_p1, 6), (force_m2, 0), (force_p2, 10)):
                if low <= p < low + part.shape[0]:
                    value = part[p - low, d] if value is None else value + part[p - low, d]
            force_s[p, d] = value * inverse

    values = v0[...] + v1[...] + v2[...] + v3[...]
    dense_s[...] = values
    rows64 = lax.broadcasted_iota(I32, (64, 128), 0)
    rows128 = lax.broadcasted_iota(I32, (128, 128), 0)
    ids = lax.broadcasted_iota(I32, (WIDE, ROWS), 0)
    for d, source in enumerate((halo_up, halo, halo_down)):
        slab_there = (j + d - 1 >= 0) & (j + d - 1 < slabs)
        lhs = []
        rhs = []
        for e in (-1, 0, 1):
            member = k + e
            there = slab_there & (member >= 0) & (member < CROSS)
            member = jnp.clip(member, 0, CROSS - 1)
            cell = source[84 + member].astype(I32)[0:1]
            amounts = dense_s[pl.ds(pl.multiple_of((d * CROSS + member) * 4, 4), 4)]
            column = (cell >> 7) & 7
            if e == 0:
                place = column
                fits = cell >= 0
            else:
                place = column + 8
                fits = (cell >= 0) & ((column < 4) if e == 1 else (column >= 4))
            place = jnp.where(fits & there, (cell >> 10) * WIDE + place, -1)
            hot = rows64 == place
            pieces = [jnp.where(hot, 1.0, 0.0).astype(BF16)]
            high = amounts.astype(BF16).astype(F32)
            rest = amounts - high
            middle = rest.astype(BF16).astype(F32)
            last = rest - middle
            for part in (high, middle, last):
                for mom in range(4):
                    pieces.append(jnp.where(hot, part[mom : mom + 1], 0.0).astype(BF16))
            lhs.append(jnp.concatenate(pieces, axis=0))
            rhs.append(jnp.where(rows128 == (cell & 127), 1.0, 0.0).astype(BF16))
        dense = lax.dot_general(
            jnp.concatenate(lhs, axis=1),
            jnp.concatenate(rhs, axis=1),
            (((1,), (1,)), ((), ())),
            preferred_element_type=F32,
        )
        outside_left = (ids >= 12) & (k == 0)
        outside_right = (ids >= 8) & (ids < 12) & (k == CROSS - 1)
        outside = outside_left | outside_right | jnp.logical_not(slab_there)
        for z in range(PLANES):
            p = d * 4 + z
            if p < 1 or p > DEEP - 2:
                continue
            low = z * WIDE

            def taken(mom):
                return (
                    dense[64 * (1 + mom) + low : 64 * (1 + mom) + low + WIDE]
                    + dense[64 * (5 + mom) + low : 64 * (5 + mom) + low + WIDE]
                    + dense[64 * (9 + mom) + low : 64 * (9 + mom) + low + WIDE]
                )

            hit_s[p] = jnp.where(outside, 1.0, dense[low : low + WIDE])
            density = taken(0)
            base, pairs = equilibrium_terms([taken(1), taken(2), taken(3)])
            edge_s[0, p] = density * base * (1.0 / 3.0)
            for n, (along, even) in enumerate(pairs):
                scaled = density * (1.0 / 18.0 if n < 3 else 1.0 / 36.0)
                edge_s[2 * n + 1, p] = scaled * (even + along)
                edge_s[2 * n + 2, p] = scaled * (even - along)

    for step in range(STEPS):
        source, dest = (f_s, g_s) if step % 2 == 0 else (g_s, f_s)

        def plane(p, carry):
            if step == 0:
                fields = [source[q, p + 1] for q in range(19)]
            else:
                hit = hit_s[p] > 0.5
                fields = [jnp.where(hit, edge_s[q, p], source[q, p + 1]) for q in range(19)]
            density, momentum = moments(fields)
            inverse = 1.0 / density
            velocity = [(momentum[d] + force_s[p, d]) * inverse for d in range(3)]
            omega = relax_s[p]
            fluid = mask_s[p] > 0.5
            keep = 1.0 - omega
            amount = omega * density
            base, pairs = equilibrium_terms(velocity)
            dest[0, p + 1] = jnp.where(
                fluid, keep * fields[0] + (amount * (1.0 / 3.0)) * base, fields[0]
            )
            light = amount * (1.0 / 18.0)
            lighter = amount * (1.0 / 36.0)
            for n, (along, even) in enumerate(pairs):
                one, two = fields[2 * n + 1], fields[2 * n + 2]
                scaled = light if n < 3 else lighter
                c = VELOCITIES[2 * n + 1]
                new_one = jnp.where(fluid, keep * one + scaled * (even + along), two)
                new_two = jnp.where(fluid, keep * two + scaled * (even - along), one)
                dest[2 * n + 1, p + 1 + c[0]] = rolled(new_one, c)
                dest[2 * n + 2, p + 1 - c[0]] = rolled(new_two, tuple(-x for x in c))
            return carry

        lax.fori_loop(step, DEEP - step, plane, 0)

    last = f_s if STEPS % 2 == 0 else g_s
    for z in range(PLANES):
        p = STEPS + z
        hit = hit_s[p, 0:8] > 0.5
        fields = [jnp.where(hit, edge_s[q, p, 0:8], last[q, p + 1, 0:8]) for q in range(19)]
        for q in range(19):
            pops_o[q, z] = fields[q]
        density, momentum = moments(fields)
        scale = ROOT_THREE / density
        for d in range(3):
            flow_o[d, z] = momentum[d] * scale


def slab_shift(value, steps):
    count = lax.axis_size("slab")
    pairs = [(s, s + steps) for s in range(count) if 0 <= s + steps < count]
    return lax.ppermute(value, "slab", pairs)


def cross_shift(value, steps):
    return lax.ppermute(value, "cross", [(s, (s + steps) % CROSS) for s in range(CROSS)])


def swap_group_and_cross(value):
    pairs = []
    for group in range(CROSS):
        for place in range(GROUP):
            for k in range(CROSS):
                pairs.append(
                    ((group * GROUP + place) * CROSS + k, (k * GROUP + place) * CROSS + group)
                )
    return lax.ppermute(value, ("slab", "cross"), pairs)


def exchange_masked(value, mask):
    return lax.ppermute(value, "slab", [(s, s ^ mask) for s in range(lax.axis_size("slab"))])


def on_device(
    populations, fluid_mask, relaxation, positions, triangles, tension, coarse_moments, interface
):
    own, to_right, to_left, iface, shard = call(
        pack_kernel,
        (struct(84, 8, ROWS), struct(43, 8, ROWS), struct(43, 8, ROWS), struct(8, ROWS), struct(4, 512)),
    )(populations, relaxation, fluid_mask, interface, coarse_moments)
    table = swap_group_and_cross(shard)
    from_left = cross_shift(to_right, 1)
    from_right = cross_shift(to_left, -1)
    iface_far = cross_shift(iface, 2)
    up = slab_shift(own, 1)
    down = slab_shift(own, -1)
    for mask in MASKS[:-1]:
        table = jnp.concatenate([table, exchange_masked(table, mask)], axis=0)
    other = exchange_masked(table, MASKS[-1])

    halo = call(halo_kernel, struct(88, 8, ROWS))(from_left, from_right, iface_far, iface)
    halo_up = slab_shift(halo, 1)
    halo_down = slab_shift(halo, -1)

    nodes = call(
        nodal_kernel,
        struct(MEMBRANES, 8, NODES),
        [pltpu.VMEM((48, NODES), F32), pltpu.VMEM((NODES, 1280), BF16)],
        flops=1 << 30,
    )(positions, triangles, tension)

    half = MEMBRANES // 2

    def half_spec(at):
        return pl.BlockSpec((half, 8, NODES), lambda i: (at, 0, 0))

    def whole_spec(*shape):
        return pl.BlockSpec(shape, lambda i: (0,) * len(shape))

    partial = call(
        spread_first_kernel,
        struct(768, ROWS),
        grid=(1,),
        in_specs=[half_spec(0)],
        out_specs=whole_spec(768, ROWS),
        flops=1 << 31,
    )(nodes)
    counts = (8, 6, 6, 2, 2)
    force, to_up, to_down, to_up2, to_down2 = call(
        spread_last_kernel,
        tuple(struct(n, 3, WIDE, ROWS) for n in counts),
        grid=(1,),
        in_specs=[half_spec(1), whole_spec(768, ROWS)],
        out_specs=tuple(whole_spec(n, 3, WIDE, ROWS) for n in counts),
        flops=1 << 31,
    )(nodes, partial)
    force_m1 = slab_shift(to_up, 1)
    force_p1 = slab_shift(to_down, -1)
    force_m2 = slab_shift(to_up2, 2)
    force_p2 = slab_shift(to_down2, -2)

    tail = pl.BlockSpec((4, 8, ROWS), lambda i: (21, 0, 0))
    found = call(
        lookup_kernel,
        struct(48, ROWS),
        grid=(1,),
        in_specs=[whole_spec(64, 512), whole_spec(64, 512), tail, tail, tail],
        out_specs=whole_spec(48, ROWS),
        flops=1 << 30,
    )(table, other, halo_up, halo, halo_down)
    found1 = cross_shift(found, 1)
    found2 = cross_shift(found, 2)
    found3 = cross_shift(found, 3)

    state = pltpu.VMEM((19, DEEP + 2, WIDE, ROWS), F32)
    field = pltpu.VMEM((DEEP, WIDE, ROWS), F32)
    return call(
        steps_kernel,
        (struct(*populations.shape), struct(3, *populations.shape[1:])),
        [
            state,
            state,
            pltpu.VMEM((19, DEEP, WIDE, ROWS), F32),
            field,
            field,
            field,
            pltpu.VMEM((DEEP, 3, WIDE, ROWS), F32),
            pltpu.VMEM((48, ROWS), F32),
        ],
        flops=1 << 31,
    )(
        populations, relaxation, fluid_mask, up, down, halo, halo_up, halo_down,
        force, force_m1, force_p1, force_m2, force_p2, found, found1, found2, found3,
    )


def solution(mesh):
    in_specs = (
        P(None, "slab", "cross", None),
        P("slab", "cross", None),
        P("slab", "cross", None),
        P(None, "slab", None),
        P(),
        P("slab", None),
        P(None, "slab"),
        P(None, ("slab", "cross")),
    )
    out_specs = (P(None, "slab", "cross", None), P(None, "slab", "cross", None))
    return jax.shard_map(
        on_device, mesh=mesh, in_specs=in_specs, out_specs=out_specs, check_vma=False
    )
```

```python
import math

import jax
import jax.numpy as jnp
from jax import lax
from jax.experimental import pallas as pl
from jax.experimental.pallas import tpu as pltpu
from jax.sharding import PartitionSpec as P

F32 = jnp.float32
BF16 = jnp.bfloat16
I32 = jnp.int32
ROOT_THREE = math.sqrt(3.0)
VELOCITIES = [
    (0, 0, 0),
    (1, 0, 0),
    (-1, 0, 0),
    (0, 1, 0),
    (0, -1, 0),
    (0, 0, 1),
    (0, 0, -1),
    (1, 1, 0),
    (-1, -1, 0),
    (1, -1, 0),
    (-1, 1, 0),
    (1, 0, 1),
    (-1, 0, -1),
    (1, 0, -1),
    (-1, 0, 1),
    (0, 1, 1),
    (0, -1, -1),
    (0, 1, -1),
    (0, -1, 1),
]
STEPS = 4
PLANES = 4
COLUMNS = 8
ROWS = 128
DEEP = PLANES + 2 * STEPS
WIDE = COLUMNS + 2 * STEPS
CROSS = 4
NODES = 768
MEMBRANES = 16


def call(body, outs, scratch=(), flops=0, limit=16, **more):
    return pl.pallas_call(
        body,
        out_shape=outs,
        scratch_shapes=list(scratch),
        compiler_params=pltpu.CompilerParams(vmem_limit_bytes=limit << 20),
        cost_estimate=pl.CostEstimate(flops=flops, bytes_accessed=1 << 20, transcendentals=0),
        **more,
    )


def struct(*shape, dtype=F32):
    return jax.ShapeDtypeStruct(shape, dtype)


def pack_kernel(pops, relax, mask, iface, right_o, left_o):
    def put(field, z, value):
        low = (z % 2) * 4
        right_o[field * 2 + z // 2, low : low + 4] = value[4:8]
        left_o[field * 2 + z // 2, low : low + 4] = value[0:4]

    for z in range(PLANES):
        for q in range(19):
            put(q, z, pops[q, z])
        put(19, z, relax[z])
        put(20, z, mask[z].astype(F32))
    for out in (right_o, left_o):
        out[42] = jnp.zeros((8, ROWS), F32)
        out[42, 0:3] = iface[...].astype(F32)


def wide_kernel(pops, relax, mask, iface, force, from_left, from_right, wide_o):
    for p in range(8):
        wide_o[86 + p * 3 : 89 + p * 3] = force[p]
    for z in range(PLANES):
        for q in range(19):
            wide_o[q * 4 + z, 0:8] = pops[q, z]
        wide_o[76 + z, 0:8] = relax[z]
        wide_o[80 + z, 0:8] = mask[z].astype(F32)
    for tile in range(42):
        right = from_right[tile]
        left = from_left[tile]
        wide_o[2 * tile, 8:12] = right[0:4]
        wide_o[2 * tile + 1, 8:12] = right[4:8]
        wide_o[2 * tile, 12:16] = left[0:4]
        wide_o[2 * tile + 1, 12:16] = left[4:8]
    wide_o[84, 0:8] = from_left[42]
    wide_o[84, 8:16] = jnp.zeros((8, ROWS), F32)
    wide_o[84, 8:11] = iface[...].astype(F32)
    wide_o[85, 0:8] = from_right[42]
    wide_o[85, 8:16] = jnp.zeros((8, ROWS), F32)


def nodal_kernel(positions, triangles, tension, out, x_s, table_s):
    j = lax.axis_index("slab")
    k = lax.axis_index("cross")
    x_s[...] = jnp.zeros_like(x_s)
    for d in range(3):
        coords = positions[d].astype(F32)
        x_s[d * 16 : d * 16 + 16, 0:642] = coords - coords[:, 0:1]
    tri = triangles[...]
    for low in range(0, NODES, 128):
        ids = lax.broadcasted_iota(I32, (128, 1280), 0) + low
        hit = (ids == tri[0:1]) | (ids == tri[1:2]) | (ids == tri[2:3])
        table_s[low : low + 128] = jnp.where(hit, 1.0, 0.0).astype(BF16)
    x = x_s[...]
    table = table_s[...]
    corners = jnp.dot(x.astype(BF16), table, preferred_element_type=F32)
    s = tension[...]
    weighted = jnp.concatenate([corners[d * 16 : d * 16 + 16] * s for d in range(3)] + [s], axis=0)
    high = weighted.astype(BF16)
    rest = weighted - high.astype(F32)
    middle = rest.astype(BF16)
    low_part = (rest - middle.astype(F32)).astype(BF16)
    stacked = jnp.concatenate([high, middle, low_part], axis=0)
    sums = lax.dot_general(stacked, table, (((1,), (1,)), ((), ())), preferred_element_type=F32)
    total = sums[0:64] + sums[64:128] + sums[128:192]
    out[...] = jnp.zeros_like(out)
    base = (j * PLANES, k * COLUMNS, 0)
    for d in range(3):
        force = total[d * 16 : d * 16 + 16] - 3.0 * x[d * 16 : d * 16 + 16] * total[48:64]
        place = (positions[d] - base[d]).astype(F32)
        for m in range(MEMBRANES):
            out[m, d : d + 1] = force[m : m + 1]
            out[m, 3 + d : 4 + d, 0:642] = place[m : m + 1]


def spread_body(nodes, initial, finished):
    plane_ids = lax.broadcasted_iota(I32, (8, NODES), 0).astype(F32) - 2.0
    column_ids = lax.broadcasted_iota(I32, (WIDE, NODES), 0)
    column_ids = jnp.where(column_ids < 12, column_ids, column_ids - 16).astype(F32)
    row_ids = (lax.broadcasted_iota(I32, (ROWS, NODES), 0).astype(F32) * 0.25).astype(BF16)

    def add(m, running):
        node = nodes[m]
        along_plane = jnp.maximum(0.5 - 0.25 * jnp.abs(plane_ids - node[3:4]), 0.0)
        along_column = jnp.maximum(0.5 - 0.25 * jnp.abs(column_ids - node[4:5]), 0.0)
        row = jnp.broadcast_to(node[5:6] * 0.25, (16, NODES)).astype(BF16)
        row = jnp.concatenate([row] * 8, axis=0)
        along_row = jnp.abs(jnp.abs(row_ids - row) - BF16(16.0))
        along_row = jnp.maximum(along_row - BF16(15.5), BF16(0.0))
        parts = []
        rest = []
        for d in range(3):
            high = node[d : d + 1].astype(BF16).astype(F32)
            parts.append((high * along_column).astype(BF16))
            rest.append(((node[d : d + 1] - high).astype(BF16).astype(F32) * along_column).astype(BF16))
        block = jnp.concatenate(parts + rest, axis=0)
        stacked = []
        for p in range(8):
            weight = jnp.broadcast_to(along_plane[p : p + 1], (16, NODES)).astype(BF16)
            stacked.append(block * jnp.concatenate([weight] * 6, axis=0))
        lhs = jnp.concatenate(stacked, axis=0)
        return running + lax.dot_general(
            lhs, along_row, (((1,), (1,)), ((), ())), preferred_element_type=F32
        )

    return lax.fori_loop(0, nodes.shape[0], add, initial)


def spread_first_kernel(nodes, out):
    out[...] = spread_body(nodes, jnp.zeros((768, ROWS), F32), None)


def spread_last_kernel(nodes, partial, own_o, up2_o, down2_o):
    total = spread_body(nodes, partial[...], None)
    for p in range(8):
        for d in range(3):
            low = p * 96 + d * 16
            value = total[low : low + 16] + total[low + 48 : low + 64]
            own_o[p, d] = value
            if p >= 6:
                up2_o[p - 6, d] = value
            if p < 2:
                down2_o[p, d] = value


def lookup_kernel(table, other, up, own, down, out):
    core = lax.rem(lax.axis_index("cross"), 2)
    slabs = table.shape[0] // 8
    lhs = []
    for part in range(2):
        for source in (table, other):
            for quarter in range(2):
                pieces = []
                for mom in range(4):
                    value = source[pl.ds(mom * 2 + quarter, slabs, stride=8)]
                    high = value.astype(BF16)
                    pieces.append(high if part == 0 else (value - high.astype(F32)).astype(BF16))
                lhs.append(jnp.concatenate(pieces, axis=0))
    lhs = jnp.concatenate(lhs, axis=1)
    ids = lax.broadcasted_iota(I32, (512, 256), 0)
    slab_ids = lax.broadcasted_iota(I32, (slabs, 256), 0)
    for d, source in enumerate((up, own, down)):
        for e in range(3):
            tile = source[e // 2, (e % 2) * 8 : (e % 2) * 8 + 8].astype(I32)
            cell = jnp.concatenate([tile[1:2], tile[2:3]], axis=1)
            hot = jnp.where(ids == ((cell & 511) ^ (core * 256)), 1.0, 0.0).astype(BF16)
            found = jnp.dot(
                lhs, jnp.concatenate([hot, hot], axis=0), preferred_element_type=F32
            )
            chosen = slab_ids == (cell >> 9)
            for mom in range(4):
                value = jnp.sum(
                    jnp.where(chosen, found[mom * slabs : (mom + 1) * slabs], 0.0),
                    axis=0,
                    keepdims=True,
                )
                at = (d * 3 + e) * 4 + mom
                out[at : at + 1] = 0.75 * value[:, 0:128] + 0.25 * value[:, 128:256]


def rolled(value, velocity):
    if velocity[1]:
        value = pltpu.roll(value, velocity[1] % WIDE, 0)
    if velocity[2]:
        value = pltpu.roll(value, velocity[2] % ROWS, 1)
    return value


def moments(fields):
    def pick(d, sign):
        return [f for f, c in zip(fields, VELOCITIES) if c[d] == sign]

    def add(values):
        while len(values) > 1:
            values = [a + b for a, b in zip(values[::2], values[1::2])] + (
                [values[-1]] if len(values) % 2 else []
            )
        return values[0]

    return add(list(fields)), [add(pick(d, 1)) - add(pick(d, -1)) for d in range(3)]


def equilibrium_terms(v):
    base = 1.0 - 1.5 * (v[0] * v[0] + v[1] * v[1] + v[2] * v[2])
    t = [3.0 * x for x in v]
    pairs = []
    for q in range(1, 19, 2):
        c = VELOCITIES[q]
        along = None
        for d in range(3):
            if c[d]:
                term = t[d]
                if along is None:
                    along = term
                else:
                    along = along + term if c[d] == 1 else along - term
        pairs.append((along, base + 0.5 * along * along))
    return base, pairs


def steps_kernel(
    own, up, down, force_m2, force_p2, found,
    pops_o, flow_o,
    f_s, g_s, edge_s, hit_s, relax_s, mask_s, force_s,
):
    j = lax.axis_index("slab")
    k = lax.axis_index("cross")
    slabs = lax.axis_size("slab")
    for low, source in ((0, up), (4, own), (8, down)):
        for q in range(19):
            f_s[q, low + 1 : low + 5] = source[q * 4 : q * 4 + 4]
        relax_s[low : low + 4] = source[76:80]
        mask_s[low : low + 4] = source[80:84]
    for p in range(DEEP):
        inverse = 1.0 / relax_s[p]
        for d in range(3):
            value = None
            for part, shift in ((own, -2), (up, 2), (down, -6)):
                if 0 <= p + shift < 8:
                    more = part[86 + (p + shift) * 3 + d]
                    value = more if value is None else value + more
            for part, low in ((force_m2, 0), (force_p2, 10)):
                if low <= p < low + 2:
                    value = value + part[p - low, d]
            force_s[p, d] = value * inverse

    rows64 = lax.broadcasted_iota(I32, (64, 128), 0)
    rows128 = lax.broadcasted_iota(I32, (128, 128), 0)
    ids = lax.broadcasted_iota(I32, (WIDE, ROWS), 0)
    for d, source in enumerate((up, own, down)):
        slab_there = (j + d - 1 >= 0) & (j + d - 1 < slabs)
        lhs = []
        rhs = []
        for e in (-1, 0, 1):
            member = k + e
            there = slab_there & (member >= 0) & (member < CROSS)
            at = e + 1
            cell = source[84 + at // 2, (at % 2) * 8 : (at % 2) * 8 + 1].astype(I32)
            amounts = found[(d * 3 + at) * 4 : (d * 3 + at) * 4 + 4]
            column = (cell >> 7) & 7
            if e == 0:
                place = column
                fits = cell >= 0
            else:
                place = column + 8
                fits = (cell >= 0) & ((column < 4) if e == 1 else (column >= 4))
            place = jnp.where(fits & there, (cell >> 10) * WIDE + place, -1)
            hot = rows64 == place
            pieces = [jnp.where(hot, 1.0, 0.0).astype(BF16)]
            high = amounts.astype(BF16).astype(F32)
            rest = amounts - high
            middle = rest.astype(BF16).astype(F32)
            last = rest - middle
            for part in (high, middle, last):
                for mom in range(4):
                    pieces.append(jnp.where(hot, part[mom : mom + 1], 0.0).astype(BF16))
            lhs.append(jnp.concatenate(pieces, axis=0))
            rhs.append(jnp.where(rows128 == (cell & 127), 1.0, 0.0).astype(BF16))
        dense = lax.dot_general(
            jnp.concatenate(lhs, axis=1),
            jnp.concatenate(rhs, axis=1),
            (((1,), (1,)), ((), ())),
            preferred_element_type=F32,
        )
        outside_left = (ids >= 12) & (k == 0)
        outside_right = (ids >= 8) & (ids < 12) & (k == CROSS - 1)
        outside = outside_left | outside_right | jnp.logical_not(slab_there)
        for z in range(PLANES):
            p = d * 4 + z
            if p < 1 or p > DEEP - 2:
                continue
            low = z * WIDE

            def taken(mom):
                return (
                    dense[64 * (1 + mom) + low : 64 * (1 + mom) + low + WIDE]
                    + dense[64 * (5 + mom) + low : 64 * (5 + mom) + low + WIDE]
                    + dense[64 * (9 + mom) + low : 64 * (9 + mom) + low + WIDE]
                )

            hit_s[p] = jnp.where(outside, 1.0, dense[low : low + WIDE])
            density = taken(0)
            base, pairs = equilibrium_terms([taken(1), taken(2), taken(3)])
            edge_s[0, p] = density * base * (1.0 / 3.0)
            for n, (along, even) in enumerate(pairs):
                scaled = density * (1.0 / 18.0 if n < 3 else 1.0 / 36.0)
                edge_s[2 * n + 1, p] = scaled * (even + along)
                edge_s[2 * n + 2, p] = scaled * (even - along)

    for step in range(STEPS):
        source, dest = (f_s, g_s) if step % 2 == 0 else (g_s, f_s)

        def plane(p, carry):
            if step == 0:
                fields = [source[q, p + 1] for q in range(19)]
            else:
                hit = hit_s[p] > 0.5
                fields = [jnp.where(hit, edge_s[q, p], source[q, p + 1]) for q in range(19)]
            density, momentum = moments(fields)
            inverse = 1.0 / density
            velocity = [(momentum[d] + force_s[p, d]) * inverse for d in range(3)]
            omega = relax_s[p]
            fluid = mask_s[p] > 0.5
            keep = 1.0 - omega
            amount = omega * density
            base, pairs = equilibrium_terms(velocity)
            dest[0, p + 1] = jnp.where(
                fluid, keep * fields[0] + (amount * (1.0 / 3.0)) * base, fields[0]
            )
            light = amount * (1.0 / 18.0)
            lighter = amount * (1.0 / 36.0)
            for n, (along, even) in enumerate(pairs):
                one, two = fields[2 * n + 1], fields[2 * n + 2]
                scaled = light if n < 3 else lighter
                c = VELOCITIES[2 * n + 1]
                new_one = jnp.where(fluid, keep * one + scaled * (even + along), two)
                new_two = jnp.where(fluid, keep * two + scaled * (even - along), one)
                dest[2 * n + 1, p + 1 + c[0]] = rolled(new_one, c)
                dest[2 * n + 2, p + 1 - c[0]] = rolled(new_two, tuple(-x for x in c))
            return carry

        lax.fori_loop(step, DEEP - step, plane, 0)

    last = f_s if STEPS % 2 == 0 else g_s
    for z in range(PLANES):
        p = STEPS + z
        hit = hit_s[p, 0:8] > 0.5
        fields = [jnp.where(hit, edge_s[q, p, 0:8], last[q, p + 1, 0:8]) for q in range(19)]
        for q in range(19):
            pops_o[q, z] = fields[q]
        density, momentum = moments(fields)
        scale = ROOT_THREE / density
        for d in range(3):
            flow_o[d, z] = momentum[d] * scale


def slab_shift(value, steps):
    count = lax.axis_size("slab")
    pairs = [(s, s + steps) for s in range(count) if 0 <= s + steps < count]
    return lax.ppermute(value, "slab", pairs)


def cross_shift(value, steps):
    pairs = [(s, s + steps) for s in range(CROSS) if 0 <= s + steps < CROSS]
    return lax.ppermute(value, "cross", pairs)


def on_device(
    populations, fluid_mask, relaxation, positions, triangles, tension, coarse_moments, interface
):
    slabs = lax.axis_size("slab")
    core = lax.rem(lax.axis_index("cross"), 2)
    shard = lax.dynamic_index_in_dim(coarse_moments.reshape(4, 2, 2, ROWS), core, 1, keepdims=False)
    shard = shard.reshape(8, ROWS)
    table = lax.all_to_all(jnp.broadcast_to(shard[None], (slabs, 8, ROWS)), "slab", 0, 0)

    fields = (populations, relaxation, fluid_mask, interface)
    to_right, to_left = call(pack_kernel, (struct(43, 8, ROWS), struct(43, 8, ROWS)))(*fields)
    from_left = cross_shift(to_right, 1)
    from_right = cross_shift(to_left, -1)
    nodes = call(
        nodal_kernel,
        struct(MEMBRANES, 8, NODES),
        [pltpu.VMEM((48, NODES), F32), pltpu.VMEM((NODES, 1280), BF16)],
        flops=1 << 30,
    )(positions, triangles, tension)

    half = MEMBRANES // 2

    def half_spec(at):
        return pl.BlockSpec((half, 8, NODES), lambda i: (at, 0, 0))

    def whole_spec(*shape):
        return pl.BlockSpec(shape, lambda i: (0,) * len(shape))

    partial = call(
        spread_first_kernel,
        struct(768, ROWS),
        grid=(1,),
        in_specs=[half_spec(0)],
        out_specs=whole_spec(768, ROWS),
        flops=1 << 31,
    )(nodes)
    counts = (8, 2, 2)
    force, to_up2, to_down2 = call(
        spread_last_kernel,
        tuple(struct(n, 3, WIDE, ROWS) for n in counts),
        grid=(1,),
        in_specs=[half_spec(1), whole_spec(768, ROWS)],
        out_specs=tuple(whole_spec(n, 3, WIDE, ROWS) for n in counts),
        flops=1 << 31,
    )(nodes, partial)
    wide = call(wide_kernel, struct(110, WIDE, ROWS))(*fields, force, from_left, from_right)
    wide_up = slab_shift(wide, 1)
    wide_down = slab_shift(wide, -1)
    force_m2 = slab_shift(to_up2, 2)
    force_p2 = slab_shift(to_down2, -2)
    other = lax.ppermute(table, "cross", [(s, s ^ 1) for s in range(CROSS)])

    tail = pl.BlockSpec((2, WIDE, ROWS), lambda i: (42, 0, 0))
    found = call(
        lookup_kernel,
        struct(36, ROWS),
        grid=(1,),
        in_specs=[whole_spec(slabs * 8, ROWS), whole_spec(slabs * 8, ROWS), tail, tail, tail],
        out_specs=whole_spec(36, ROWS),
        flops=1 << 30,
    )(table.reshape(slabs * 8, ROWS), other.reshape(slabs * 8, ROWS), wide_up, wide, wide_down)

    state = pltpu.VMEM((19, DEEP + 2, WIDE, ROWS), F32)
    field = pltpu.VMEM((DEEP, WIDE, ROWS), F32)
    return call(
        steps_kernel,
        (struct(*populations.shape), struct(3, *populations.shape[1:])),
        [
            state,
            state,
            pltpu.VMEM((19, DEEP, WIDE, ROWS), F32),
            field,
            field,
            field,
            pltpu.VMEM((DEEP, 3, WIDE, ROWS), F32),
        ],
        flops=1 << 31,
    )(
        wide, wide_up, wide_down, force_m2, force_p2, found
    )


def solution(mesh):
    in_specs = (
        P(None, "slab", "cross", None),
        P("slab", "cross", None),
        P("slab", "cross", None),
        P(None, "slab", None),
        P(),
        P("slab", None),
        P(None, "slab"),
        P(None, ("slab", "cross")),
    )
    out_specs = (P(None, "slab", "cross", None), P(None, "slab", "cross", None))
    return jax.shard_map(
        on_device, mesh=mesh, in_specs=in_specs, out_specs=out_specs, check_vma=False
    )
```

```python
import math

import jax
import jax.numpy as jnp
from jax import lax
from jax.experimental import pallas as pl
from jax.experimental.pallas import tpu as pltpu
from jax.sharding import PartitionSpec as P

F32 = jnp.float32
BF16 = jnp.bfloat16
I32 = jnp.int32
ROOT_THREE = math.sqrt(3.0)
VELOCITIES = [
    (0, 0, 0),
    (1, 0, 0),
    (-1, 0, 0),
    (0, 1, 0),
    (0, -1, 0),
    (0, 0, 1),
    (0, 0, -1),
    (1, 1, 0),
    (-1, -1, 0),
    (1, -1, 0),
    (-1, 1, 0),
    (1, 0, 1),
    (-1, 0, -1),
    (1, 0, -1),
    (-1, 0, 1),
    (0, 1, 1),
    (0, -1, -1),
    (0, 1, -1),
    (0, -1, 1),
]
STEPS = 4
PLANES = 4
COLUMNS = 8
ROWS = 128
DEEP = PLANES + 2 * STEPS
WIDE = COLUMNS + 2 * STEPS
CROSS = 4
NODES = 768
MEMBRANES = 16


def call(body, outs, scratch=(), flops=0, limit=16, **more):
    return pl.pallas_call(
        body,
        out_shape=outs,
        scratch_shapes=list(scratch),
        compiler_params=pltpu.CompilerParams(vmem_limit_bytes=limit << 20),
        cost_estimate=pl.CostEstimate(flops=flops, bytes_accessed=1 << 20, transcendentals=0),
        **more,
    )


def struct(*shape, dtype=F32):
    return jax.ShapeDtypeStruct(shape, dtype)


def pack_kernel(pops, relax, mask, iface, right_o, left_o):
    def put(field, z, value):
        low = (z % 2) * 4
        right_o[field * 2 + z // 2, low : low + 4] = value[4:8]
        left_o[field * 2 + z // 2, low : low + 4] = value[0:4]

    for z in range(PLANES):
        for q in range(19):
            put(q, z, pops[q, z])
        put(19, z, relax[z])
        put(20, z, mask[z].astype(F32))
    for out in (right_o, left_o):
        out[42] = jnp.zeros((8, ROWS), F32)
        out[42, 0:3] = iface[...].astype(F32)


def wide_kernel(pops, relax, mask, iface, force, from_left, from_right, wide_o):
    for p in range(8):
        wide_o[86 + p * 3 : 89 + p * 3] = force[p]
    for z in range(PLANES):
        for q in range(19):
            wide_o[q * 4 + z, 0:8] = pops[q, z]
        wide_o[76 + z, 0:8] = relax[z]
        wide_o[80 + z, 0:8] = mask[z].astype(F32)
    for tile in range(42):
        right = from_right[tile]
        left = from_left[tile]
        wide_o[2 * tile, 8:12] = right[0:4]
        wide_o[2 * tile + 1, 8:12] = right[4:8]
        wide_o[2 * tile, 12:16] = left[0:4]
        wide_o[2 * tile + 1, 12:16] = left[4:8]
    wide_o[84, 0:8] = from_left[42]
    wide_o[84, 8:16] = jnp.zeros((8, ROWS), F32)
    wide_o[84, 8:11] = iface[...].astype(F32)
    wide_o[85, 0:8] = from_right[42]
    wide_o[85, 8:16] = jnp.zeros((8, ROWS), F32)


def nodal_kernel(positions, triangles, tension, out, x_s, table_s):
    j = lax.axis_index("slab")
    k = lax.axis_index("cross")
    x_s[...] = jnp.zeros_like(x_s)
    for d in range(3):
        coords = positions[d].astype(F32)
        x_s[d * 16 : d * 16 + 16, 0:642] = coords - coords[:, 0:1]
    tri = triangles[...]
    for low in range(0, NODES, 128):
        ids = lax.broadcasted_iota(I32, (128, 1280), 0) + low
        hit = (ids == tri[0:1]) | (ids == tri[1:2]) | (ids == tri[2:3])
        table_s[low : low + 128] = jnp.where(hit, 1.0, 0.0).astype(BF16)
    x = x_s[...]
    table = table_s[...]
    corners = jnp.dot(x.astype(BF16), table, preferred_element_type=F32)
    s = tension[...]
    weighted = jnp.concatenate([corners[d * 16 : d * 16 + 16] * s for d in range(3)] + [s], axis=0)
    high = weighted.astype(BF16)
    rest = weighted - high.astype(F32)
    middle = rest.astype(BF16)
    low_part = (rest - middle.astype(F32)).astype(BF16)
    stacked = jnp.concatenate([high, middle, low_part], axis=0)
    sums = lax.dot_general(stacked, table, (((1,), (1,)), ((), ())), preferred_element_type=F32)
    total = sums[0:64] + sums[64:128] + sums[128:192]
    out[...] = jnp.zeros_like(out)
    base = (j * PLANES, k * COLUMNS, 0)
    for d in range(3):
        force = total[d * 16 : d * 16 + 16] - 3.0 * x[d * 16 : d * 16 + 16] * total[48:64]
        place = (positions[d] - base[d]).astype(F32)
        for m in range(MEMBRANES):
            out[m, d : d + 1] = force[m : m + 1]
            out[m, 3 + d : 4 + d, 0:642] = place[m : m + 1]


def spread_body(nodes, initial, finished):
    plane_ids = lax.broadcasted_iota(I32, (8, NODES), 0).astype(F32) - 2.0
    column_ids = lax.broadcasted_iota(I32, (WIDE, NODES), 0)
    column_ids = jnp.where(column_ids < 12, column_ids, column_ids - 16).astype(F32)
    row_ids = (lax.broadcasted_iota(I32, (ROWS, NODES), 0).astype(F32) * 0.25).astype(BF16)

    def add(m, running):
        node = nodes[m]
        along_plane = jnp.maximum(0.5 - 0.25 * jnp.abs(plane_ids - node[3:4]), 0.0)
        along_column = jnp.maximum(0.5 - 0.25 * jnp.abs(column_ids - node[4:5]), 0.0)
        row = jnp.broadcast_to(node[5:6] * 0.25, (16, NODES)).astype(BF16)
        row = jnp.concatenate([row] * 8, axis=0)
        along_row = jnp.abs(jnp.abs(row_ids - row) - BF16(16.0))
        along_row = jnp.maximum(along_row - BF16(15.5), BF16(0.0))
        parts = []
        rest = []
        for d in range(3):
            high = node[d : d + 1].astype(BF16).astype(F32)
            parts.append((high * along_column).astype(BF16))
            rest.append(((node[d : d + 1] - high).astype(BF16).astype(F32) * along_column).astype(BF16))
        block = jnp.concatenate(parts + rest, axis=0)
        stacked = []
        for p in range(8):
            weight = jnp.broadcast_to(along_plane[p : p + 1], (16, NODES)).astype(BF16)
            stacked.append(block * jnp.concatenate([weight] * 6, axis=0))
        lhs = jnp.concatenate(stacked, axis=0)
        return running + lax.dot_general(
            lhs, along_row, (((1,), (1,)), ((), ())), preferred_element_type=F32
        )

    return lax.fori_loop(0, nodes.shape[0], add, initial, unroll=True)


def spread_first_kernel(nodes, out):
    out[...] = spread_body(nodes, jnp.zeros((768, ROWS), F32), None)


def spread_last_kernel(nodes, partial, own_o, up2_o, down2_o):
    total = spread_body(nodes, partial[...], None)
    for p in range(8):
        for d in range(3):
            low = p * 96 + d * 16
            value = total[low : low + 16] + total[low + 48 : low + 64]
            own_o[p, d] = value
            if p >= 6:
                up2_o[p - 6, d] = value
            if p < 2:
                down2_o[p, d] = value


def chunk_kernel(coarse, out):
    core = lax.rem(lax.axis_index("cross"), 2)
    rows = []
    for mom in range(4):
        for quarter in range(2):
            low = pl.multiple_of(core * 256 + quarter * 128, 128)
            rows.append(coarse[mom : mom + 1, pl.ds(low, 128)])
    tile = jnp.concatenate(rows, axis=0)
    out[...] = jnp.broadcast_to(tile[None], out.shape)


def lookup(lhs, source, out, at):
    core = lax.rem(lax.axis_index("cross"), 2)
    slabs = lhs.shape[0] // 4
    ids = lax.broadcasted_iota(I32, (512, 256), 0)
    slab_ids = lax.broadcasted_iota(I32, (slabs, 256), 0)
    for e in range(3):
        tile = source[e // 2, (e % 2) * 8 : (e % 2) * 8 + 8].astype(I32)
        cell = jnp.concatenate([tile[1:2], tile[2:3]], axis=1)
        hot = jnp.where(ids == ((cell & 511) ^ (core * 256)), 1.0, 0.0).astype(BF16)
        found = jnp.dot(lhs, jnp.concatenate([hot, hot], axis=0), preferred_element_type=F32)
        chosen = slab_ids == (cell >> 9)
        for mom in range(4):
            value = jnp.sum(
                jnp.where(chosen, found[mom * slabs : (mom + 1) * slabs], 0.0),
                axis=0,
                keepdims=True,
            )
            row = at + e * 4 + mom
            out[row : row + 1] = 0.75 * value[:, 0:128] + 0.25 * value[:, 128:256]


def lookup_own_kernel(table, other, own, out, lhs_o):
    slabs = table.shape[0] // 8
    lhs = []
    for part in range(2):
        for source in (table, other):
            for quarter in range(2):
                pieces = []
                for mom in range(4):
                    value = source[pl.ds(mom * 2 + quarter, slabs, stride=8)]
                    high = value.astype(BF16)
                    pieces.append(high if part == 0 else (value - high.astype(F32)).astype(BF16))
                lhs.append(jnp.concatenate(pieces, axis=0))
    lhs = jnp.concatenate(lhs, axis=1)
    lhs_o[...] = lhs
    lookup(lhs, own, out, 0)


def lookup_far_kernel(lhs, up, down, out):
    lookup(lhs[...], up, out, 0)
    lookup(lhs[...], down, out, 12)


def rolled(value, velocity):
    if velocity[1]:
        value = pltpu.roll(value, velocity[1] % WIDE, 0)
    if velocity[2]:
        value = pltpu.roll(value, velocity[2] % ROWS, 1)
    return value


def moments(fields):
    def pick(d, sign):
        return [f for f, c in zip(fields, VELOCITIES) if c[d] == sign]

    def add(values):
        while len(values) > 1:
            values = [a + b for a, b in zip(values[::2], values[1::2])] + (
                [values[-1]] if len(values) % 2 else []
            )
        return values[0]

    return add(list(fields)), [add(pick(d, 1)) - add(pick(d, -1)) for d in range(3)]


def equilibrium_terms(v):
    base = 1.0 - 1.5 * (v[0] * v[0] + v[1] * v[1] + v[2] * v[2])
    t = [3.0 * x for x in v]
    pairs = []
    for q in range(1, 19, 2):
        c = VELOCITIES[q]
        along = None
        for d in range(3):
            if c[d]:
                term = t[d]
                if along is None:
                    along = term
                else:
                    along = along + term if c[d] == 1 else along - term
        pairs.append((along, base + 0.5 * along * along))
    return base, pairs


def steps_kernel(
    own, up, down, force_m2, force_p2, found_own, found_far,
    pops_o, flow_o,
    f_s, g_s, edge_s, hit_s, relax_s, mask_s, force_s,
):
    j = lax.axis_index("slab")
    k = lax.axis_index("cross")
    slabs = lax.axis_size("slab")
    for low, source in ((0, up), (4, own), (8, down)):
        for q in range(19):
            f_s[q, low + 1 : low + 5] = source[q * 4 : q * 4 + 4]
        relax_s[low : low + 4] = source[76:80]
        mask_s[low : low + 4] = source[80:84]
    for p in range(DEEP):
        inverse = 1.0 / relax_s[p]
        for d in range(3):
            value = None
            for part, shift in ((own, -2), (up, 2), (down, -6)):
                if 0 <= p + shift < 8:
                    more = part[86 + (p + shift) * 3 + d]
                    value = more if value is None else value + more
            for part, low in ((force_m2, 0), (force_p2, 10)):
                if low <= p < low + 2:
                    value = value + part[p - low, d]
            force_s[p, d] = value * inverse

    rows64 = lax.broadcasted_iota(I32, (64, 128), 0)
    rows128 = lax.broadcasted_iota(I32, (128, 128), 0)
    ids = lax.broadcasted_iota(I32, (WIDE, ROWS), 0)
    founds = ((found_far, 0), (found_own, 0), (found_far, 12))
    for d, source in enumerate((up, own, down)):
        found, found_at = founds[d]
        slab_there = (j + d - 1 >= 0) & (j + d - 1 < slabs)
        lhs = []
        rhs = []
        for e in (-1, 0, 1):
            member = k + e
            there = slab_there & (member >= 0) & (member < CROSS)
            at = e + 1
            cell = source[84 + at // 2, (at % 2) * 8 : (at % 2) * 8 + 1].astype(I32)
            amounts = found[found_at + at * 4 : found_at + at * 4 + 4]
            column = (cell >> 7) & 7
            if e == 0:
                place = column
                fits = cell >= 0
            else:
                place = column + 8
                fits = (cell >= 0) & ((column < 4) if e == 1 else (column >= 4))
            place = jnp.where(fits & there, (cell >> 10) * WIDE + place, -1)
            hot = rows64 == place
            pieces = [jnp.where(hot, 1.0, 0.0).astype(BF16)]
            high = amounts.astype(BF16).astype(F32)
            rest = amounts - high
            middle = rest.astype(BF16).astype(F32)
            last = rest - middle
            for part in (high, middle, last):
                for mom in range(4):
                    pieces.append(jnp.where(hot, part[mom : mom + 1], 0.0).astype(BF16))
            lhs.append(jnp.concatenate(pieces, axis=0))
            rhs.append(jnp.where(rows128 == (cell & 127), 1.0, 0.0).astype(BF16))
        dense = lax.dot_general(
            jnp.concatenate(lhs, axis=1),
            jnp.concatenate(rhs, axis=1),
            (((1,), (1,)), ((), ())),
            preferred_element_type=F32,
        )
        outside_left = (ids >= 12) & (k == 0)
        outside_right = (ids >= 8) & (ids < 12) & (k == CROSS - 1)
        outside = outside_left | outside_right | jnp.logical_not(slab_there)
        for z in range(PLANES):
            p = d * 4 + z
            if p < 1 or p > DEEP - 2:
                continue
            low = z * WIDE

            def taken(mom):
                return (
                    dense[64 * (1 + mom) + low : 64 * (1 + mom) + low + WIDE]
                    + dense[64 * (5 + mom) + low : 64 * (5 + mom) + low + WIDE]
                    + dense[64 * (9 + mom) + low : 64 * (9 + mom) + low + WIDE]
                )

            hit_s[p] = jnp.where(outside, 1.0, dense[low : low + WIDE])
            density = taken(0)
            base, pairs = equilibrium_terms([taken(1), taken(2), taken(3)])
            edge_s[0, p] = density * base * (1.0 / 3.0)
            for n, (along, even) in enumerate(pairs):
                scaled = density * (1.0 / 18.0 if n < 3 else 1.0 / 36.0)
                edge_s[2 * n + 1, p] = scaled * (even + along)
                edge_s[2 * n + 2, p] = scaled * (even - along)

    for step in range(STEPS):
        source, dest = (f_s, g_s) if step % 2 == 0 else (g_s, f_s)

        def plane(p, carry):
            if step == 0:
                fields = [source[q, p + 1] for q in range(19)]
            else:
                hit = hit_s[p] > 0.5
                fields = [jnp.where(hit, edge_s[q, p], source[q, p + 1]) for q in range(19)]
            density, momentum = moments(fields)
            inverse = 1.0 / density
            velocity = [(momentum[d] + force_s[p, d]) * inverse for d in range(3)]
            omega = relax_s[p]
            fluid = mask_s[p] > 0.5
            keep = 1.0 - omega
            amount = omega * density
            base, pairs = equilibrium_terms(velocity)
            dest[0, p + 1] = jnp.where(
                fluid, keep * fields[0] + (amount * (1.0 / 3.0)) * base, fields[0]
            )
            light = amount * (1.0 / 18.0)
            lighter = amount * (1.0 / 36.0)
            for n, (along, even) in enumerate(pairs):
                one, two = fields[2 * n + 1], fields[2 * n + 2]
                scaled = light if n < 3 else lighter
                c = VELOCITIES[2 * n + 1]
                new_one = jnp.where(fluid, keep * one + scaled * (even + along), two)
                new_two = jnp.where(fluid, keep * two + scaled * (even - along), one)
                dest[2 * n + 1, p + 1 + c[0]] = rolled(new_one, c)
                dest[2 * n + 2, p + 1 - c[0]] = rolled(new_two, tuple(-x for x in c))
            return carry

        lax.fori_loop(step, DEEP - step, plane, 0, unroll=2)

    last = f_s if STEPS % 2 == 0 else g_s
    for z in range(PLANES):
        p = STEPS + z
        hit = hit_s[p, 0:8] > 0.5
        fields = [jnp.where(hit, edge_s[q, p, 0:8], last[q, p + 1, 0:8]) for q in range(19)]
        for q in range(19):
            pops_o[q, z] = fields[q]
        density, momentum = moments(fields)
        scale = ROOT_THREE / density
        for d in range(3):
            flow_o[d, z] = momentum[d] * scale


def slab_shift(value, steps):
    count = lax.axis_size("slab")
    pairs = [(s, s + steps) for s in range(count) if 0 <= s + steps < count]
    return lax.ppermute(value, "slab", pairs)


def cross_shift(value, steps):
    pairs = [(s, s + steps) for s in range(CROSS) if 0 <= s + steps < CROSS]
    return lax.ppermute(value, "cross", pairs)


def on_device(
    populations, fluid_mask, relaxation, positions, triangles, tension, coarse_moments, interface
):
    slabs = lax.axis_size("slab")
    table = lax.all_to_all(
        call(chunk_kernel, struct(slabs, 8, ROWS))(coarse_moments), "slab", 0, 0
    )

    fields = (populations, relaxation, fluid_mask, interface)
    to_right, to_left = call(pack_kernel, (struct(43, 8, ROWS), struct(43, 8, ROWS)))(*fields)
    from_left = cross_shift(to_right, 1)
    from_right = cross_shift(to_left, -1)
    nodes = call(
        nodal_kernel,
        struct(MEMBRANES, 8, NODES),
        [pltpu.VMEM((48, NODES), F32), pltpu.VMEM((NODES, 1280), BF16)],
        flops=1 << 30,
    )(positions, triangles, tension)

    half = MEMBRANES // 2

    def half_spec(at):
        return pl.BlockSpec((half, 8, NODES), lambda i: (at, 0, 0))

    def whole_spec(*shape):
        return pl.BlockSpec(shape, lambda i: (0,) * len(shape))

    partial = call(
        spread_first_kernel,
        struct(768, ROWS),
        grid=(1,),
        in_specs=[half_spec(0)],
        out_specs=whole_spec(768, ROWS),
        flops=1 << 31,
    )(nodes)
    counts = (8, 2, 2)
    force, to_up2, to_down2 = call(
        spread_last_kernel,
        tuple(struct(n, 3, WIDE, ROWS) for n in counts),
        grid=(1,),
        in_specs=[half_spec(1), whole_spec(768, ROWS)],
        out_specs=tuple(whole_spec(n, 3, WIDE, ROWS) for n in counts),
        flops=1 << 31,
    )(nodes, partial)
    wide = call(wide_kernel, struct(110, WIDE, ROWS))(*fields, force, from_left, from_right)
    wide_up = slab_shift(wide, 1)
    wide_down = slab_shift(wide, -1)
    force_m2 = slab_shift(to_up2, 2)
    force_p2 = slab_shift(to_down2, -2)
    other = lax.ppermute(table, "cross", [(s, s ^ 1) for s in range(CROSS)])

    tail = pl.BlockSpec((2, WIDE, ROWS), lambda i: (42, 0, 0))
    found_own, lhs = call(
        lookup_own_kernel,
        (struct(12, ROWS), struct(4 * slabs, 1024, dtype=BF16)),
        grid=(1,),
        in_specs=[whole_spec(slabs * 8, ROWS), whole_spec(slabs * 8, ROWS), tail],
        out_specs=(whole_spec(12, ROWS), whole_spec(4 * slabs, 1024)),
        flops=1 << 30,
    )(table.reshape(slabs * 8, ROWS), other.reshape(slabs * 8, ROWS), wide)
    found_far = call(
        lookup_far_kernel,
        struct(24, ROWS),
        grid=(1,),
        in_specs=[whole_spec(4 * slabs, 1024), tail, tail],
        out_specs=whole_spec(24, ROWS),
        flops=1 << 30,
    )(lhs, wide_up, wide_down)

    state = pltpu.VMEM((19, DEEP + 2, WIDE, ROWS), F32)
    field = pltpu.VMEM((DEEP, WIDE, ROWS), F32)
    return call(
        steps_kernel,
        (struct(*populations.shape), struct(3, *populations.shape[1:])),
        [
            state,
            state,
            pltpu.VMEM((19, DEEP, WIDE, ROWS), F32),
            field,
            field,
            field,
            pltpu.VMEM((DEEP, 3, WIDE, ROWS), F32),
        ],
        flops=1 << 31,
    )(
        wide, wide_up, wide_down, force_m2, force_p2, found_own, found_far
    )


def solution(mesh):
    in_specs = (
        P(None, "slab", "cross", None),
        P("slab", "cross", None),
        P("slab", "cross", None),
        P(None, "slab", None),
        P(),
        P("slab", None),
        P(None, "slab"),
        P(None, ("slab", "cross")),
    )
    out_specs = (P(None, "slab", "cross", None), P(None, "slab", "cross", None))
    return jax.shard_map(
        on_device, mesh=mesh, in_specs=in_specs, out_specs=out_specs, check_vma=False
    )
```

```python
import math

import jax
import jax.numpy as jnp
from jax import lax
from jax.experimental import pallas as pl
from jax.experimental.pallas import tpu as pltpu
from jax.sharding import PartitionSpec as P

F32 = jnp.float32
BF16 = jnp.bfloat16
I32 = jnp.int32
ROOT_THREE = math.sqrt(3.0)
VELOCITIES = [
    (0, 0, 0),
    (1, 0, 0),
    (-1, 0, 0),
    (0, 1, 0),
    (0, -1, 0),
    (0, 0, 1),
    (0, 0, -1),
    (1, 1, 0),
    (-1, -1, 0),
    (1, -1, 0),
    (-1, 1, 0),
    (1, 0, 1),
    (-1, 0, -1),
    (1, 0, -1),
    (-1, 0, 1),
    (0, 1, 1),
    (0, -1, -1),
    (0, 1, -1),
    (0, -1, 1),
]
STEPS = 4
PLANES = 4
COLUMNS = 8
ROWS = 128
DEEP = PLANES + 2 * STEPS
WIDE = COLUMNS + 2 * STEPS
CROSS = 4
RISING = [q for q, c in enumerate(VELOCITIES) if c[0] == 1]
FALLING = [q for q, c in enumerate(VELOCITIES) if c[0] == -1]
FULL, FAR, RELAX, MASK, FORCE, TILES = 2, 59, 68, 72, 76, 91
NODES = 768
MEMBRANES = 16


def call(body, outs, scratch=(), flops=0, limit=16, **more):
    return pl.pallas_call(
        body,
        out_shape=outs,
        scratch_shapes=list(scratch),
        compiler_params=pltpu.CompilerParams(vmem_limit_bytes=limit << 20),
        cost_estimate=pl.CostEstimate(flops=flops, bytes_accessed=1 << 20, transcendentals=0),
        **more,
    )


def struct(*shape, dtype=F32):
    return jax.ShapeDtypeStruct(shape, dtype)


def pack_kernel(pops, relax, mask, iface, right_o, left_o):
    def put(field, z, value):
        low = (z % 2) * 4
        right_o[field * 2 + z // 2, low : low + 4] = value[4:8]
        left_o[field * 2 + z // 2, low : low + 4] = value[0:4]

    for z in range(PLANES):
        for q in range(19):
            put(q, z, pops[q, z])
        put(19, z, relax[z])
        put(20, z, mask[z].astype(F32))
    for out in (right_o, left_o):
        out[42] = jnp.zeros((8, ROWS), F32)
        out[42, 0:3] = iface[...].astype(F32)


def wide_kernel(pops, relax, mask, iface, force, from_left, from_right, wide_o, up_o, down_o):
    for p in range(8):
        wide_o[86 + p * 3 : 89 + p * 3] = force[p]
    for z in range(PLANES):
        for q in range(19):
            wide_o[q * 4 + z, 0:8] = pops[q, z]
        wide_o[76 + z, 0:8] = relax[z]
        wide_o[80 + z, 0:8] = mask[z].astype(F32)
    for tile in range(42):
        right = from_right[tile]
        left = from_left[tile]
        wide_o[2 * tile, 8:12] = right[0:4]
        wide_o[2 * tile + 1, 8:12] = right[4:8]
        wide_o[2 * tile, 12:16] = left[0:4]
        wide_o[2 * tile + 1, 12:16] = left[4:8]
    wide_o[84, 0:8] = from_left[42]
    wide_o[84, 8:16] = jnp.zeros((8, ROWS), F32)
    wide_o[84, 8:11] = iface[...].astype(F32)
    wide_o[85, 0:8] = from_right[42]
    wide_o[85, 8:16] = jnp.zeros((8, ROWS), F32)
    for out, far, near, carried, first in ((up_o, 0, 1, RISING, 2), (down_o, 3, 0, FALLING, 5)):
        out[0:FULL] = wide_o[84:86]
        for q in range(19):
            out[FULL + q * 3 : FULL + q * 3 + 3] = wide_o[q * 4 + near : q * 4 + near + 3]
        fields = [wide_o[q * 4 + far] for q in range(19)]
        fluid = wide_o[80 + far] > 0.5
        for n, q in enumerate(carried):
            out[FAR + n] = jnp.where(fluid, fields[q], fields[opposite(q)])
        density, momentum = moments(fields)
        inverse = 1.0 / wide_o[76 + far]
        out[FAR + 5] = density
        for d in range(3):
            out[FAR + 6 + d] = momentum[d] + force[first, d] * inverse
        out[RELAX:FORCE] = wide_o[76:84]
        low = 3 if first == 2 else 0
        for p in range(5):
            out[FORCE + p * 3 : FORCE + p * 3 + 3] = force[low + p]


def opposite(q):
    return 0 if q == 0 else q + 1 if q % 2 else q - 1


def nodal_kernel(positions, triangles, tension, out, x_s, table_s):
    j = lax.axis_index("slab")
    k = lax.axis_index("cross")
    x_s[...] = jnp.zeros_like(x_s)
    for d in range(3):
        coords = positions[d].astype(F32)
        x_s[d * 16 : d * 16 + 16, 0:642] = coords - coords[:, 0:1]
    tri = triangles[...]
    for low in range(0, NODES, 128):
        ids = lax.broadcasted_iota(I32, (128, 1280), 0) + low
        hit = (ids == tri[0:1]) | (ids == tri[1:2]) | (ids == tri[2:3])
        table_s[low : low + 128] = jnp.where(hit, 1.0, 0.0).astype(BF16)
    x = x_s[...]
    table = table_s[...]
    corners = jnp.dot(x.astype(BF16), table, preferred_element_type=F32)
    s = tension[...]
    weighted = jnp.concatenate([corners[d * 16 : d * 16 + 16] * s for d in range(3)] + [s], axis=0)
    high = weighted.astype(BF16)
    rest = weighted - high.astype(F32)
    middle = rest.astype(BF16)
    low_part = (rest - middle.astype(F32)).astype(BF16)
    stacked = jnp.concatenate([high, middle, low_part], axis=0)
    sums = lax.dot_general(stacked, table, (((1,), (1,)), ((), ())), preferred_element_type=F32)
    total = sums[0:64] + sums[64:128] + sums[128:192]
    out[...] = jnp.zeros_like(out)
    base = (j * PLANES, k * COLUMNS, 0)
    for d in range(3):
        force = total[d * 16 : d * 16 + 16] - 3.0 * x[d * 16 : d * 16 + 16] * total[48:64]
        place = (positions[d] - base[d]).astype(F32)
        for m in range(MEMBRANES):
            out[m, d : d + 1] = force[m : m + 1]
            out[m, 3 + d : 4 + d, 0:642] = place[m : m + 1]


def spread_body(nodes, initial, finished):
    plane_ids = lax.broadcasted_iota(I32, (8, NODES), 0).astype(F32) - 2.0
    column_ids = lax.broadcasted_iota(I32, (WIDE, NODES), 0)
    column_ids = jnp.where(column_ids < 12, column_ids, column_ids - 16).astype(F32)
    row_ids = (lax.broadcasted_iota(I32, (ROWS, NODES), 0).astype(F32) * 0.25).astype(BF16)

    def add(m, running):
        node = nodes[m]
        along_plane = jnp.maximum(0.5 - 0.25 * jnp.abs(plane_ids - node[3:4]), 0.0)
        along_column = jnp.maximum(0.5 - 0.25 * jnp.abs(column_ids - node[4:5]), 0.0)
        row = jnp.broadcast_to(node[5:6] * 0.25, (16, NODES)).astype(BF16)
        row = jnp.concatenate([row] * 8, axis=0)
        along_row = jnp.abs(jnp.abs(row_ids - row) - BF16(16.0))
        along_row = jnp.maximum(along_row - BF16(15.5), BF16(0.0))
        parts = []
        rest = []
        for d in range(3):
            high = node[d : d + 1].astype(BF16).astype(F32)
            parts.append((high * along_column).astype(BF16))
            rest.append(((node[d : d + 1] - high).astype(BF16).astype(F32) * along_column).astype(BF16))
        block = jnp.concatenate(parts + rest, axis=0)
        stacked = []
        for p in range(8):
            weight = jnp.broadcast_to(along_plane[p : p + 1], (16, NODES)).astype(BF16)
            stacked.append(block * jnp.concatenate([weight] * 6, axis=0))
        lhs = jnp.concatenate(stacked, axis=0)
        return running + lax.dot_general(
            lhs, along_row, (((1,), (1,)), ((), ())), preferred_element_type=F32
        )

    return lax.fori_loop(0, nodes.shape[0], add, initial, unroll=True)


def spread_first_kernel(nodes, out):
    out[...] = spread_body(nodes, jnp.zeros((768, ROWS), F32), None)


def spread_last_kernel(nodes, partial, own_o, up2_o, down2_o):
    total = spread_body(nodes, partial[...], None)
    for p in range(8):
        for d in range(3):
            low = p * 96 + d * 16
            value = total[low : low + 16] + total[low + 48 : low + 64]
            own_o[p, d] = value
            if p >= 6:
                up2_o[p - 6, d] = value
            if p < 2:
                down2_o[p, d] = value


def chunk_kernel(coarse, out):
    core = lax.rem(lax.axis_index("cross"), 2)
    rows = []
    for mom in range(4):
        for quarter in range(2):
            low = pl.multiple_of(core * 256 + quarter * 128, 128)
            rows.append(coarse[mom : mom + 1, pl.ds(low, 128)])
    tile = jnp.concatenate(rows, axis=0)
    out[...] = jnp.broadcast_to(tile[None], out.shape)


def lookup(lhs, source, out, at):
    core = lax.rem(lax.axis_index("cross"), 2)
    slabs = lhs.shape[0] // 4
    ids = lax.broadcasted_iota(I32, (512, 256), 0)
    slab_ids = lax.broadcasted_iota(I32, (slabs, 256), 0)
    for e in range(3):
        tile = source[e // 2, (e % 2) * 8 : (e % 2) * 8 + 8].astype(I32)
        cell = jnp.concatenate([tile[1:2], tile[2:3]], axis=1)
        hot = jnp.where(ids == ((cell & 511) ^ (core * 256)), 1.0, 0.0).astype(BF16)
        found = jnp.dot(lhs, jnp.concatenate([hot, hot], axis=0), preferred_element_type=F32)
        chosen = slab_ids == (cell >> 9)
        for mom in range(4):
            value = jnp.sum(
                jnp.where(chosen, found[mom * slabs : (mom + 1) * slabs], 0.0),
                axis=0,
                keepdims=True,
            )
            row = at + e * 4 + mom
            out[row : row + 1] = 0.75 * value[:, 0:128] + 0.25 * value[:, 128:256]


def lookup_own_kernel(table, other, own, out, lhs_o):
    slabs = table.shape[0] // 8
    lhs = []
    for part in range(2):
        for source in (table, other):
            for quarter in range(2):
                pieces = []
                for mom in range(4):
                    value = source[pl.ds(mom * 2 + quarter, slabs, stride=8)]
                    high = value.astype(BF16)
                    pieces.append(high if part == 0 else (value - high.astype(F32)).astype(BF16))
                lhs.append(jnp.concatenate(pieces, axis=0))
    lhs = jnp.concatenate(lhs, axis=1)
    lhs_o[...] = lhs
    lookup(lhs, own, out, 0)


def lookup_far_kernel(lhs, up, down, out):
    lookup(lhs[...], up, out, 0)
    lookup(lhs[...], down, out, 12)


def rolled(value, velocity):
    if velocity[1]:
        value = pltpu.roll(value, velocity[1] % WIDE, 0)
    if velocity[2]:
        value = pltpu.roll(value, velocity[2] % ROWS, 1)
    return value


def moments(fields):
    def pick(d, sign):
        return [f for f, c in zip(fields, VELOCITIES) if c[d] == sign]

    def add(values):
        while len(values) > 1:
            values = [a + b for a, b in zip(values[::2], values[1::2])] + (
                [values[-1]] if len(values) % 2 else []
            )
        return values[0]

    return add(list(fields)), [add(pick(d, 1)) - add(pick(d, -1)) for d in range(3)]


def equilibrium_terms(v):
    base = 1.0 - 1.5 * (v[0] * v[0] + v[1] * v[1] + v[2] * v[2])
    t = [3.0 * x for x in v]
    pairs = []
    for q in range(1, 19, 2):
        c = VELOCITIES[q]
        along = None
        for d in range(3):
            if c[d]:
                term = t[d]
                if along is None:
                    along = term
                else:
                    along = along + term if c[d] == 1 else along - term
        pairs.append((along, base + 0.5 * along * along))
    return base, pairs


def steps_kernel(
    own, up, down, force_m2, force_p2, found_own, found_far,
    pops_o, flow_o,
    f_s, g_s, edge_s, hit_s, force_s,
):
    j = lax.axis_index("slab")
    k = lax.axis_index("cross")
    slabs = lax.axis_size("slab")

    def tile(p, own_at, far_at):
        part = p // 4
        return own[own_at + p % 4] if part == 1 else (up, None, down)[part][far_at + p % 4]

    def relaxation_of(p):
        return tile(p, 76, RELAX)

    def fluid_of(p):
        return tile(p, 80, MASK) > 0.5

    for p in range(DEEP):
        inverse = 1.0 / relaxation_of(p)
        for d in range(3):
            parts = []
            if 2 <= p < 10:
                parts.append(own[86 + (p - 2) * 3 + d])
            if 1 <= p < 6:
                parts.append(up[FORCE + (p - 1) * 3 + d])
            if 6 <= p < 11:
                parts.append(down[FORCE + (p - 6) * 3 + d])
            if p < 2:
                parts.append(force_m2[p, d])
            if p >= 10:
                parts.append(force_p2[p - 10, d])
            force_s[p, d] = sum(parts[1:], parts[0]) * inverse

    rows64 = lax.broadcasted_iota(I32, (64, 128), 0)
    rows128 = lax.broadcasted_iota(I32, (128, 128), 0)
    ids = lax.broadcasted_iota(I32, (WIDE, ROWS), 0)
    founds = ((found_far, 0), (found_own, 0), (found_far, 12))
    for d, source in enumerate((up, own, down)):
        found, found_at = founds[d]
        slab_there = (j + d - 1 >= 0) & (j + d - 1 < slabs)
        lhs = []
        rhs = []
        for e in (-1, 0, 1):
            member = k + e
            there = slab_there & (member >= 0) & (member < CROSS)
            at = e + 1
            tile_at = (84 if d == 1 else 0) + at // 2
            cell = source[tile_at, (at % 2) * 8 : (at % 2) * 8 + 1].astype(I32)
            amounts = found[found_at + at * 4 : found_at + at * 4 + 4]
            column = (cell >> 7) & 7
            if e == 0:
                place = column
                fits = cell >= 0
            else:
                place = column + 8
                fits = (cell >= 0) & ((column < 4) if e == 1 else (column >= 4))
            place = jnp.where(fits & there, (cell >> 10) * WIDE + place, -1)
            hot = rows64 == place
            pieces = [jnp.where(hot, 1.0, 0.0).astype(BF16)]
            high = amounts.astype(BF16).astype(F32)
            rest = amounts - high
            middle = rest.astype(BF16).astype(F32)
            last = rest - middle
            for part in (high, middle, last):
                for mom in range(4):
                    pieces.append(jnp.where(hot, part[mom : mom + 1], 0.0).astype(BF16))
            lhs.append(jnp.concatenate(pieces, axis=0))
            rhs.append(jnp.where(rows128 == (cell & 127), 1.0, 0.0).astype(BF16))
        dense = lax.dot_general(
            jnp.concatenate(lhs, axis=1),
            jnp.concatenate(rhs, axis=1),
            (((1,), (1,)), ((), ())),
            preferred_element_type=F32,
        )
        outside_left = (ids >= 12) & (k == 0)
        outside_right = (ids >= 8) & (ids < 12) & (k == CROSS - 1)
        outside = outside_left | outside_right | jnp.logical_not(slab_there)
        for z in range(PLANES):
            p = d * 4 + z
            if p < 1 or p > DEEP - 2:
                continue
            low = z * WIDE

            def taken(mom):
                return (
                    dense[64 * (1 + mom) + low : 64 * (1 + mom) + low + WIDE]
                    + dense[64 * (5 + mom) + low : 64 * (5 + mom) + low + WIDE]
                    + dense[64 * (9 + mom) + low : 64 * (9 + mom) + low + WIDE]
                )

            hit_s[p] = jnp.where(outside, 1.0, dense[low : low + WIDE])
            density = taken(0)
            base, pairs = equilibrium_terms([taken(1), taken(2), taken(3)])
            edge_s[0, p] = density * base * (1.0 / 3.0)
            for n, (along, even) in enumerate(pairs):
                scaled = density * (1.0 / 18.0 if n < 3 else 1.0 / 36.0)
                edge_s[2 * n + 1, p] = scaled * (even + along)
                edge_s[2 * n + 2, p] = scaled * (even - along)

    def collide(p, fields, density, momentum, wanted, put):
        inverse = 1.0 / density
        velocity = [(momentum[d] + force_s[p, d]) * inverse for d in range(3)]
        omega = relaxation_of(p)
        fluid = fluid_of(p)
        keep = 1.0 - omega
        amount = omega * density
        base, pairs = equilibrium_terms(velocity)
        if 0 in wanted:
            put(0, jnp.where(fluid, keep * fields[0] + (amount * (1.0 / 3.0)) * base, fields[0]))
        light = amount * (1.0 / 18.0)
        lighter = amount * (1.0 / 36.0)
        for n, (along, even) in enumerate(pairs):
            scaled = light if n < 3 else lighter
            for q in (2 * n + 1, 2 * n + 2):
                if q in wanted:
                    toward = even + along if q % 2 else even - along
                    put(q, jnp.where(fluid, keep * fields[q] + scaled * toward, fields[opposite(q)]))

    for step in range(STEPS):
        source, dest = (f_s, g_s) if step % 2 == 0 else (g_s, f_s)
        for p in range(step, DEEP - step):

            def put(q, value, p=p, dest=dest):
                c = VELOCITIES[q]
                dest[q, p + 1 + c[0]] = rolled(value, c)

            wanted = [q for q, c in enumerate(VELOCITIES) if step < p + c[0] < DEEP - 1 - step]
            if step == 0 and p in (0, DEEP - 1):
                message, carried = (up, RISING) if p == 0 else (down, FALLING)
                fields = {}
                for n, q in enumerate(carried):
                    fields[q] = fields[opposite(q)] = message[FAR + n]
                moved = [message[FAR + 6 + d] for d in range(3)]
                collide(p, fields, message[FAR + 5], moved, wanted, put)
                continue
            if step == 0:
                if p // 4 == 1:
                    fields = [own[q * 4 + p % 4] for q in range(19)]
                else:
                    message, near = (up, p - 1) if p < 4 else (down, p - 8)
                    fields = [message[FULL + q * 3 + near] for q in range(19)]
            else:
                hit = hit_s[p] > 0.5
                fields = [jnp.where(hit, edge_s[q, p], source[q, p + 1]) for q in range(19)]
            density, momentum = moments(fields)
            collide(p, fields, density, momentum, wanted, put)

    last = f_s if STEPS % 2 == 0 else g_s
    for z in range(PLANES):
        p = STEPS + z
        hit = hit_s[p, 0:8] > 0.5
        fields = [jnp.where(hit, edge_s[q, p, 0:8], last[q, p + 1, 0:8]) for q in range(19)]
        for q in range(19):
            pops_o[q, z] = fields[q]
        density, momentum = moments(fields)
        scale = ROOT_THREE / density
        for d in range(3):
            flow_o[d, z] = momentum[d] * scale


def slab_shift(value, steps):
    count = lax.axis_size("slab")
    pairs = [(s, s + steps) for s in range(count) if 0 <= s + steps < count]
    return lax.ppermute(value, "slab", pairs)


def cross_shift(value, steps):
    pairs = [(s, s + steps) for s in range(CROSS) if 0 <= s + steps < CROSS]
    return lax.ppermute(value, "cross", pairs)


def on_device(
    populations, fluid_mask, relaxation, positions, triangles, tension, coarse_moments, interface
):
    slabs = lax.axis_size("slab")
    table = lax.all_to_all(
        call(chunk_kernel, struct(slabs, 8, ROWS))(coarse_moments), "slab", 0, 0
    )

    fields = (populations, relaxation, fluid_mask, interface)
    to_right, to_left = call(pack_kernel, (struct(43, 8, ROWS), struct(43, 8, ROWS)))(*fields)
    from_left = cross_shift(to_right, 1)
    from_right = cross_shift(to_left, -1)
    nodes = call(
        nodal_kernel,
        struct(MEMBRANES, 8, NODES),
        [pltpu.VMEM((48, NODES), F32), pltpu.VMEM((NODES, 1280), BF16)],
        flops=1 << 30,
    )(positions, triangles, tension)

    half = MEMBRANES // 2

    def half_spec(at):
        return pl.BlockSpec((half, 8, NODES), lambda i: (at, 0, 0))

    def whole_spec(*shape):
        return pl.BlockSpec(shape, lambda i: (0,) * len(shape))

    partial = call(
        spread_first_kernel,
        struct(768, ROWS),
        grid=(1,),
        in_specs=[half_spec(0)],
        out_specs=whole_spec(768, ROWS),
        flops=1 << 31,
    )(nodes)
    counts = (8, 2, 2)
    force, to_up2, to_down2 = call(
        spread_last_kernel,
        tuple(struct(n, 3, WIDE, ROWS) for n in counts),
        grid=(1,),
        in_specs=[half_spec(1), whole_spec(768, ROWS)],
        out_specs=tuple(whole_spec(n, 3, WIDE, ROWS) for n in counts),
        flops=1 << 31,
    )(nodes, partial)
    message = struct(TILES, WIDE, ROWS)
    wide, for_up, for_down = call(wide_kernel, (struct(110, WIDE, ROWS), message, message))(
        *fields, force, from_left, from_right
    )
    wide_up = slab_shift(for_up, 1)
    wide_down = slab_shift(for_down, -1)
    force_m2 = slab_shift(to_up2, 2)
    force_p2 = slab_shift(to_down2, -2)
    other = lax.ppermute(table, "cross", [(s, s ^ 1) for s in range(CROSS)])

    tail = pl.BlockSpec((2, WIDE, ROWS), lambda i: (42, 0, 0))
    head = pl.BlockSpec((2, WIDE, ROWS), lambda i: (0, 0, 0))
    found_own, lhs = call(
        lookup_own_kernel,
        (struct(12, ROWS), struct(4 * slabs, 1024, dtype=BF16)),
        grid=(1,),
        in_specs=[whole_spec(slabs * 8, ROWS), whole_spec(slabs * 8, ROWS), tail],
        out_specs=(whole_spec(12, ROWS), whole_spec(4 * slabs, 1024)),
        flops=1 << 30,
    )(table.reshape(slabs * 8, ROWS), other.reshape(slabs * 8, ROWS), wide)
    found_far = call(
        lookup_far_kernel,
        struct(24, ROWS),
        grid=(1,),
        in_specs=[whole_spec(4 * slabs, 1024), head, head],
        out_specs=whole_spec(24, ROWS),
        flops=1 << 30,
    )(lhs, wide_up, wide_down)

    state = pltpu.VMEM((19, DEEP + 2, WIDE, ROWS), F32)
    field = pltpu.VMEM((DEEP, WIDE, ROWS), F32)
    return call(
        steps_kernel,
        (struct(*populations.shape), struct(3, *populations.shape[1:])),
        [
            state,
            state,
            pltpu.VMEM((19, DEEP, WIDE, ROWS), F32),
            field,
            pltpu.VMEM((DEEP, 3, WIDE, ROWS), F32),
        ],
        flops=1 << 31,
    )(
        wide, wide_up, wide_down, force_m2, force_p2, found_own, found_far
    )


def solution(mesh):
    in_specs = (
        P(None, "slab", "cross", None),
        P("slab", "cross", None),
        P("slab", "cross", None),
        P(None, "slab", None),
        P(),
        P("slab", None),
        P(None, "slab"),
        P(None, ("slab", "cross")),
    )
    out_specs = (P(None, "slab", "cross", None), P(None, "slab", "cross", None))
    return jax.shard_map(
        on_device, mesh=mesh, in_specs=in_specs, out_specs=out_specs, check_vma=False
    )
```

```python
import math

import jax
import jax.numpy as jnp
from jax import lax
from jax.experimental import pallas as pl
from jax.experimental.pallas import tpu as pltpu
from jax.sharding import PartitionSpec as P

F32 = jnp.float32
BF16 = jnp.bfloat16
I32 = jnp.int32
ROOT_THREE = math.sqrt(3.0)
VELOCITIES = [
    (0, 0, 0),
    (1, 0, 0),
    (-1, 0, 0),
    (0, 1, 0),
    (0, -1, 0),
    (0, 0, 1),
    (0, 0, -1),
    (1, 1, 0),
    (-1, -1, 0),
    (1, -1, 0),
    (-1, 1, 0),
    (1, 0, 1),
    (-1, 0, -1),
    (1, 0, -1),
    (-1, 0, 1),
    (0, 1, 1),
    (0, -1, -1),
    (0, 1, -1),
    (0, -1, 1),
]
STEPS = 4
PLANES = 4
COLUMNS = 8
ROWS = 128
DEEP = PLANES + 2 * STEPS
WIDE = COLUMNS + 2 * STEPS
CROSS = 4
RISING = [q for q, c in enumerate(VELOCITIES) if c[0] == 1]
FALLING = [q for q, c in enumerate(VELOCITIES) if c[0] == -1]
FULL, FAR, RELAX, MASK, FORCE, TILES = 2, 59, 68, 72, 76, 91
NODES = 768
MEMBRANES = 16


def call(body, outs, scratch=(), flops=0, limit=16, **more):
    return pl.pallas_call(
        body,
        out_shape=outs,
        scratch_shapes=list(scratch),
        compiler_params=pltpu.CompilerParams(vmem_limit_bytes=limit << 20),
        cost_estimate=pl.CostEstimate(flops=flops, bytes_accessed=1 << 20, transcendentals=0),
        **more,
    )


def struct(*shape, dtype=F32):
    return jax.ShapeDtypeStruct(shape, dtype)


def on_even_member():
    return lax.rem(lax.axis_index("cross"), 2) == 0


def pack_kernel(pops, relax, mask, iface, core_o, chip_o):
    even = on_even_member()

    def put(field, z, value):
        low = (z % 2) * 4
        core_o[field * 2 + z // 2, low : low + 4] = jnp.where(even, value[4:8], value[0:4])
        chip_o[field * 2 + z // 2, low : low + 4] = jnp.where(even, value[0:4], value[4:8])

    for z in range(PLANES):
        for q in range(19):
            put(q, z, pops[q, z])
        put(19, z, relax[z])
        put(20, z, mask[z].astype(F32))
    for out in (core_o, chip_o):
        out[42] = jnp.zeros((8, ROWS), F32)
        out[42, 0:3] = iface[...].astype(F32)


def wide_kernel(pops, relax, mask, iface, force, from_core, from_chip, up_o, down_o, first_o, wide_o):
    for z in range(PLANES):
        for q in range(19):
            wide_o[q * 4 + z, 0:8] = pops[q, z]
        wide_o[76 + z, 0:8] = relax[z]
        wide_o[80 + z, 0:8] = mask[z].astype(F32)
    even = on_even_member()

    def sides(tile):
        one, two = from_core[tile], from_chip[tile]
        return jnp.where(even, two, one), jnp.where(even, one, two)

    for tile in range(42):
        left, right = sides(tile)
        wide_o[2 * tile, 8:12] = right[0:4]
        wide_o[2 * tile + 1, 8:12] = right[4:8]
        wide_o[2 * tile, 12:16] = left[0:4]
        wide_o[2 * tile + 1, 12:16] = left[4:8]
    left, right = sides(42)
    wide_o[84, 0:8] = left
    wide_o[84, 8:16] = jnp.zeros((8, ROWS), F32)
    wide_o[84, 8:11] = iface[...].astype(F32)
    wide_o[85, 0:8] = right
    wide_o[85, 8:16] = jnp.zeros((8, ROWS), F32)
    for q in range(19):
        first_o[q] = wide_o[q * 4]
    for out, far, near, carried, first in ((up_o, 0, 1, RISING, 2), (down_o, 3, 0, FALLING, 5)):
        out[0:FULL] = wide_o[84:86]
        for q in range(19):
            out[FULL + q * 3 : FULL + q * 3 + 3] = wide_o[q * 4 + near : q * 4 + near + 3]
        fields = [wide_o[q * 4 + far] for q in range(19)]
        fluid = wide_o[80 + far] > 0.5
        for n, q in enumerate(carried):
            out[FAR + n] = jnp.where(fluid, fields[q], fields[opposite(q)])
        density, momentum = moments(fields)
        inverse = 1.0 / wide_o[76 + far]
        out[FAR + 5] = density
        for d in range(3):
            out[FAR + 6 + d] = momentum[d] + force[first, d] * inverse
        out[RELAX:FORCE] = wide_o[76:84]
        low = 3 if first == 2 else 0
        for p in range(5):
            out[FORCE + p * 3 : FORCE + p * 3 + 3] = force[low + p]


def opposite(q):
    return 0 if q == 0 else q + 1 if q % 2 else q - 1


def nodal_kernel(positions, triangles, tension, out, x_s, table_s):
    j = lax.axis_index("slab")
    k = lax.axis_index("cross")
    x_s[...] = jnp.zeros_like(x_s)
    for d in range(3):
        coords = positions[d].astype(F32)
        x_s[d * 16 : d * 16 + 16, 0:642] = coords - coords[:, 0:1]
    tri = triangles[...]
    for low in range(0, NODES, 128):
        ids = lax.broadcasted_iota(I32, (128, 1280), 0) + low
        hit = (ids == tri[0:1]) | (ids == tri[1:2]) | (ids == tri[2:3])
        table_s[low : low + 128] = jnp.where(hit, 1.0, 0.0).astype(BF16)
    x = x_s[...]
    table = table_s[...]
    corners = jnp.dot(x.astype(BF16), table, preferred_element_type=F32)
    s = tension[...]
    weighted = jnp.concatenate([corners[d * 16 : d * 16 + 16] * s for d in range(3)] + [s], axis=0)
    high = weighted.astype(BF16)
    rest = weighted - high.astype(F32)
    middle = rest.astype(BF16)
    low_part = (rest - middle.astype(F32)).astype(BF16)
    stacked = jnp.concatenate([high, middle, low_part], axis=0)
    sums = lax.dot_general(stacked, table, (((1,), (1,)), ((), ())), preferred_element_type=F32)
    total = sums[0:64] + sums[64:128] + sums[128:192]
    out[...] = jnp.zeros_like(out)
    base = (j * PLANES, k * COLUMNS, 0)
    for d in range(3):
        force = total[d * 16 : d * 16 + 16] - 3.0 * x[d * 16 : d * 16 + 16] * total[48:64]
        place = (positions[d] - base[d]).astype(F32)
        for m in range(MEMBRANES):
            out[m, d : d + 1] = force[m : m + 1]
            out[m, 3 + d : 4 + d, 0:642] = place[m : m + 1]


def spread_body(nodes):
    plane_ids = lax.broadcasted_iota(I32, (8, NODES), 0).astype(F32) - 2.0
    column_ids = lax.broadcasted_iota(I32, (WIDE, NODES), 0)
    column_ids = jnp.where(column_ids < 12, column_ids, column_ids - 16).astype(F32)
    row_ids = (lax.broadcasted_iota(I32, (ROWS, NODES), 0).astype(F32) * 0.25).astype(BF16)

    def add(m, running):
        node = nodes[m]
        along_plane = jnp.maximum(0.5 - 0.25 * jnp.abs(plane_ids - node[3:4]), 0.0)
        along_column = jnp.maximum(0.5 - 0.25 * jnp.abs(column_ids - node[4:5]), 0.0)
        row = jnp.broadcast_to(node[5:6] * 0.25, (16, NODES)).astype(BF16)
        row = jnp.concatenate([row] * 8, axis=0)
        along_row = jnp.abs(jnp.abs(row_ids - row) - BF16(16.0))
        along_row = jnp.maximum(along_row - BF16(15.5), BF16(0.0))
        parts = []
        rest = []
        for d in range(3):
            high = node[d : d + 1].astype(BF16).astype(F32)
            parts.append((high * along_column).astype(BF16))
            rest.append(((node[d : d + 1] - high).astype(BF16).astype(F32) * along_column).astype(BF16))
        block = jnp.concatenate(parts + rest, axis=0)
        stacked = []
        for p in range(8):
            weight = jnp.broadcast_to(along_plane[p : p + 1], (16, NODES)).astype(BF16)
            stacked.append(block * jnp.concatenate([weight] * 6, axis=0))
        lhs = jnp.concatenate(stacked, axis=0)
        return running + lax.dot_general(
            lhs, along_row, (((1,), (1,)), ((), ())), preferred_element_type=F32
        )

    initial = jnp.zeros((768, ROWS), F32)
    return lax.fori_loop(0, nodes.shape[0], add, initial, unroll=True)


def spread_kernel(nodes, own_o, up2_o, down2_o):
    total = spread_body(nodes)
    for p in range(8):
        for d in range(3):
            low = p * 96 + d * 16
            value = total[low : low + 16] + total[low + 48 : low + 64]
            own_o[p, d] = value
            if p >= 6:
                up2_o[p - 6, d] = value
            if p < 2:
                down2_o[p, d] = value


def chunk_kernel(coarse, out):
    core = lax.rem(lax.axis_index("cross"), 2)
    rows = []
    for mom in range(4):
        for quarter in range(2):
            low = pl.multiple_of(core * 256 + quarter * 128, 128)
            rows.append(coarse[mom : mom + 1, pl.ds(low, 128)])
    tile = jnp.concatenate(rows, axis=0)
    out[...] = jnp.broadcast_to(tile[None], out.shape)


def lookup(lhs, source, out, at):
    core = lax.rem(lax.axis_index("cross"), 2)
    slabs = lhs.shape[0] // 4
    ids = lax.broadcasted_iota(I32, (512, 256), 0)
    slab_ids = lax.broadcasted_iota(I32, (slabs, 256), 0)
    for e in range(3):
        tile = source[e // 2, (e % 2) * 8 : (e % 2) * 8 + 8].astype(I32)
        cell = jnp.concatenate([tile[1:2], tile[2:3]], axis=1)
        hot = jnp.where(ids == ((cell & 511) ^ (core * 256)), 1.0, 0.0).astype(BF16)
        found = jnp.dot(lhs, jnp.concatenate([hot, hot], axis=0), preferred_element_type=F32)
        chosen = slab_ids == (cell >> 9)
        for mom in range(4):
            value = jnp.sum(
                jnp.where(chosen, found[mom * slabs : (mom + 1) * slabs], 0.0),
                axis=0,
                keepdims=True,
            )
            row = at + e * 4 + mom
            out[row : row + 1] = 0.75 * value[:, 0:128] + 0.25 * value[:, 128:256]


def lookup_own_kernel(table, other, own, out, lhs_o):
    slabs = table.shape[0] // 8
    lhs = []
    for part in range(2):
        for source in (table, other):
            for quarter in range(2):
                pieces = []
                for mom in range(4):
                    value = source[pl.ds(mom * 2 + quarter, slabs, stride=8)]
                    high = value.astype(BF16)
                    pieces.append(high if part == 0 else (value - high.astype(F32)).astype(BF16))
                lhs.append(jnp.concatenate(pieces, axis=0))
    lhs = jnp.concatenate(lhs, axis=1)
    lhs_o[...] = lhs
    lookup(lhs, own, out, 0)


def lookup_far_kernel(lhs, up, down, out):
    lookup(lhs[...], up, out, 0)
    lookup(lhs[...], down, out, 12)


def rolled(value, velocity):
    if velocity[1]:
        value = pltpu.roll(value, velocity[1] % WIDE, 0)
    if velocity[2]:
        value = pltpu.roll(value, velocity[2] % ROWS, 1)
    return value


def moments(fields):
    def pick(d, sign):
        return [f for f, c in zip(fields, VELOCITIES) if c[d] == sign]

    def add(values):
        while len(values) > 1:
            values = [a + b for a, b in zip(values[::2], values[1::2])] + (
                [values[-1]] if len(values) % 2 else []
            )
        return values[0]

    return add(list(fields)), [add(pick(d, 1)) - add(pick(d, -1)) for d in range(3)]


def equilibrium_terms(v):
    base = 1.0 - 1.5 * (v[0] * v[0] + v[1] * v[1] + v[2] * v[2])
    t = [3.0 * x for x in v]
    pairs = []
    for q in range(1, 19, 2):
        c = VELOCITIES[q]
        along = None
        for d in range(3):
            if c[d]:
                term = t[d]
                if along is None:
                    along = term
                else:
                    along = along + term if c[d] == 1 else along - term
        pairs.append((along, base + 0.5 * along * along))
    return base, pairs


def steps_kernel(
    own_up, first_plane, up, down, force, force_m2, force_p2, found_own, found_far,
    pops_o, flow_o,
    f_s, g_s, edge_s, hit_s, force_s,
):
    j = lax.axis_index("slab")
    k = lax.axis_index("cross")
    slabs = lax.axis_size("slab")

    def tile(p, at):
        return (up, own_up, down)[p // 4][at + p % 4]

    def relaxation_of(p):
        return tile(p, RELAX)

    def fluid_of(p):
        return tile(p, MASK) > 0.5

    for p in range(DEEP):
        inverse = 1.0 / relaxation_of(p)
        for d in range(3):
            parts = []
            if 2 <= p < 10:
                parts.append(force[p - 2, d])
            if 1 <= p < 6:
                parts.append(up[FORCE + (p - 1) * 3 + d])
            if 6 <= p < 11:
                parts.append(down[FORCE + (p - 6) * 3 + d])
            if p < 2:
                parts.append(force_m2[p, d])
            if p >= 10:
                parts.append(force_p2[p - 10, d])
            force_s[p, d] = sum(parts[1:], parts[0]) * inverse

    rows64 = lax.broadcasted_iota(I32, (64, 128), 0)
    rows128 = lax.broadcasted_iota(I32, (128, 128), 0)
    ids = lax.broadcasted_iota(I32, (WIDE, ROWS), 0)
    founds = ((found_far, 0), (found_own, 0), (found_far, 12))
    for d, source in enumerate((up, own_up, down)):
        found, found_at = founds[d]
        slab_there = (j + d - 1 >= 0) & (j + d - 1 < slabs)
        lhs = []
        rhs = []
        for e in (-1, 0, 1):
            member = k + e
            there = slab_there & (member >= 0) & (member < CROSS)
            at = e + 1
            cell = source[at // 2, (at % 2) * 8 : (at % 2) * 8 + 1].astype(I32)
            amounts = found[found_at + at * 4 : found_at + at * 4 + 4]
            column = (cell >> 7) & 7
            if e == 0:
                place = column
                fits = cell >= 0
            else:
                place = column + 8
                fits = (cell >= 0) & ((column < 4) if e == 1 else (column >= 4))
            place = jnp.where(fits & there, (cell >> 10) * WIDE + place, -1)
            hot = rows64 == place
            pieces = [jnp.where(hot, 1.0, 0.0).astype(BF16)]
            high = amounts.astype(BF16).astype(F32)
            rest = amounts - high
            middle = rest.astype(BF16).astype(F32)
            last = rest - middle
            for part in (high, middle, last):
                for mom in range(4):
                    pieces.append(jnp.where(hot, part[mom : mom + 1], 0.0).astype(BF16))
            lhs.append(jnp.concatenate(pieces, axis=0))
            rhs.append(jnp.where(rows128 == (cell & 127), 1.0, 0.0).astype(BF16))
        dense = lax.dot_general(
            jnp.concatenate(lhs, axis=1),
            jnp.concatenate(rhs, axis=1),
            (((1,), (1,)), ((), ())),
            preferred_element_type=F32,
        )
        outside_left = (ids >= 12) & (k == 0)
        outside_right = (ids >= 8) & (ids < 12) & (k == CROSS - 1)
        outside = outside_left | outside_right | jnp.logical_not(slab_there)
        for z in range(PLANES):
            p = d * 4 + z
            if p < 1 or p > DEEP - 2:
                continue
            low = z * WIDE

            def taken(mom):
                return (
                    dense[64 * (1 + mom) + low : 64 * (1 + mom) + low + WIDE]
                    + dense[64 * (5 + mom) + low : 64 * (5 + mom) + low + WIDE]
                    + dense[64 * (9 + mom) + low : 64 * (9 + mom) + low + WIDE]
                )

            hit_s[p] = jnp.where(outside, 1.0, dense[low : low + WIDE])
            density = taken(0)
            base, pairs = equilibrium_terms([taken(1), taken(2), taken(3)])
            edge_s[0, p] = density * base * (1.0 / 3.0)
            for n, (along, even) in enumerate(pairs):
                scaled = density * (1.0 / 18.0 if n < 3 else 1.0 / 36.0)
                edge_s[2 * n + 1, p] = scaled * (even + along)
                edge_s[2 * n + 2, p] = scaled * (even - along)

    def collide(p, fields, density, momentum, wanted, put):
        inverse = 1.0 / density
        velocity = [(momentum[d] + force_s[p, d]) * inverse for d in range(3)]
        omega = relaxation_of(p)
        fluid = fluid_of(p)
        keep = 1.0 - omega
        amount = omega * density
        base, pairs = equilibrium_terms(velocity)
        if 0 in wanted:
            put(0, jnp.where(fluid, keep * fields[0] + (amount * (1.0 / 3.0)) * base, fields[0]))
        light = amount * (1.0 / 18.0)
        lighter = amount * (1.0 / 36.0)
        for n, (along, even) in enumerate(pairs):
            scaled = light if n < 3 else lighter
            for q in (2 * n + 1, 2 * n + 2):
                if q in wanted:
                    toward = even + along if q % 2 else even - along
                    put(q, jnp.where(fluid, keep * fields[q] + scaled * toward, fields[opposite(q)]))

    for step in range(STEPS):
        source, dest = (f_s, g_s) if step % 2 == 0 else (g_s, f_s)
        for p in range(step, DEEP - step):

            def put(q, value, p=p, dest=dest):
                c = VELOCITIES[q]
                dest[q, p + 1 + c[0]] = rolled(value, c)

            wanted = [q for q, c in enumerate(VELOCITIES) if step < p + c[0] < DEEP - 1 - step]
            if step == 0 and p in (0, DEEP - 1):
                message, carried = (up, RISING) if p == 0 else (down, FALLING)
                fields = {}
                for n, q in enumerate(carried):
                    fields[q] = fields[opposite(q)] = message[FAR + n]
                moved = [message[FAR + 6 + d] for d in range(3)]
                collide(p, fields, message[FAR + 5], moved, wanted, put)
                continue
            if step == 0:
                if p < 4:
                    message, near = up, p - 1
                elif p < 8:
                    message, near = own_up, p - 5
                else:
                    message, near = down, p - 8
                if p == 4:
                    fields = [first_plane[q] for q in range(19)]
                else:
                    fields = [message[FULL + q * 3 + near] for q in range(19)]
            else:
                hit = hit_s[p] > 0.5
                fields = [jnp.where(hit, edge_s[q, p], source[q, p + 1]) for q in range(19)]
            density, momentum = moments(fields)
            collide(p, fields, density, momentum, wanted, put)

    last = f_s if STEPS % 2 == 0 else g_s
    for z in range(PLANES):
        p = STEPS + z
        hit = hit_s[p, 0:8] > 0.5
        fields = [jnp.where(hit, edge_s[q, p, 0:8], last[q, p + 1, 0:8]) for q in range(19)]
        for q in range(19):
            pops_o[q, z] = fields[q]
        density, momentum = moments(fields)
        scale = ROOT_THREE / density
        for d in range(3):
            flow_o[d, z] = momentum[d] * scale


def slab_shift(value, steps):
    count = lax.axis_size("slab")
    pairs = [(s, s + steps) for s in range(count) if 0 <= s + steps < count]
    return lax.ppermute(value, "slab", pairs)


def cross_swap(value, first):
    pairs = []
    for s in range(first, CROSS - 1, 2):
        pairs += [(s, s + 1), (s + 1, s)]
    return lax.ppermute(value, "cross", pairs)


def on_device(
    populations, fluid_mask, relaxation, positions, triangles, tension, coarse_moments, interface
):
    slabs = lax.axis_size("slab")
    table = lax.all_to_all(
        call(chunk_kernel, struct(slabs, 8, ROWS))(coarse_moments), "slab", 0, 0
    )

    fields = (populations, relaxation, fluid_mask, interface)
    to_core, to_chip = call(pack_kernel, (struct(43, 8, ROWS), struct(43, 8, ROWS)))(*fields)
    from_core = cross_swap(to_core, 0)
    from_chip = cross_swap(to_chip, 1)
    nodes = call(
        nodal_kernel,
        struct(MEMBRANES, 8, NODES),
        [pltpu.VMEM((48, NODES), F32), pltpu.VMEM((NODES, 1280), BF16)],
        flops=1 << 30,
    )(positions, triangles, tension)

    def whole_spec(*shape):
        return pl.BlockSpec(shape, lambda i: (0,) * len(shape))

    counts = (8, 2, 2)
    force, to_up2, to_down2 = call(
        spread_kernel,
        tuple(struct(n, 3, WIDE, ROWS) for n in counts),
        grid=(1,),
        in_specs=[whole_spec(MEMBRANES, 8, NODES)],
        out_specs=tuple(whole_spec(n, 3, WIDE, ROWS) for n in counts),
        flops=1 << 31,
    )(nodes)
    message = struct(TILES, WIDE, ROWS)
    for_up, for_down, first_plane = call(
        wide_kernel, (message, message, struct(19, WIDE, ROWS)), [pltpu.VMEM((86, WIDE, ROWS), F32)]
    )(*fields, force, from_core, from_chip)
    wide_up = slab_shift(for_up, 1)
    wide_down = slab_shift(for_down, -1)
    force_m2 = slab_shift(to_up2, 2)
    force_p2 = slab_shift(to_down2, -2)
    other = cross_swap(table, 0)

    head = pl.BlockSpec((2, WIDE, ROWS), lambda i: (0, 0, 0))
    found_own, lhs = call(
        lookup_own_kernel,
        (struct(12, ROWS), struct(4 * slabs, 1024, dtype=BF16)),
        grid=(1,),
        in_specs=[whole_spec(slabs * 8, ROWS), whole_spec(slabs * 8, ROWS), head],
        out_specs=(whole_spec(12, ROWS), whole_spec(4 * slabs, 1024)),
        flops=1 << 30,
    )(table.reshape(slabs * 8, ROWS), other.reshape(slabs * 8, ROWS), for_up)
    found_far = call(
        lookup_far_kernel,
        struct(24, ROWS),
        grid=(1,),
        in_specs=[whole_spec(4 * slabs, 1024), head, head],
        out_specs=whole_spec(24, ROWS),
        flops=1 << 30,
    )(lhs, wide_up, wide_down)

    state = pltpu.VMEM((19, DEEP + 2, WIDE, ROWS), F32)
    field = pltpu.VMEM((DEEP, WIDE, ROWS), F32)
    return call(
        steps_kernel,
        (struct(*populations.shape), struct(3, *populations.shape[1:])),
        [
            state,
            state,
            pltpu.VMEM((19, DEEP, WIDE, ROWS), F32),
            field,
            pltpu.VMEM((DEEP, 3, WIDE, ROWS), F32),
        ],
        flops=1 << 31,
    )(
        for_up, first_plane, wide_up, wide_down, force, force_m2, force_p2, found_own, found_far
    )


def solution(mesh):
    in_specs = (
        P(None, "slab", "cross", None),
        P("slab", "cross", None),
        P("slab", "cross", None),
        P(None, "slab", None),
        P(),
        P("slab", None),
        P(None, "slab"),
        P(None, ("slab", "cross")),
    )
    out_specs = (P(None, "slab", "cross", None), P(None, "slab", "cross", None))
    return jax.shard_map(
        on_device, mesh=mesh, in_specs=in_specs, out_specs=out_specs, check_vma=False
    )
```
